32 devices in a mesh: cell: 8 (over z, x), spot: 4 (over y, core).
Axes of the slice: x: 2, y: 2, z: 4, core: 2. Of those that a mesh axis runs over, the one named last changes fastest.
Arguments:
- logits: float32 [16384, 4096], P('cell', 'spot'), may hold values from -8 to 8
- expression: float32 [16384, 2048], P('cell'), may hold values from -6 to 6
- spatial: float32 [2048, 4096], P('cell', 'spot'), may hold values from -6 to 6
- masks: int32 [4, 2048], replicated, may hold values 0 or 1
- slide_ids: int32 [4096], P('spot'), may hold values from 0 to 3
- counts: int32 [4], replicated, may hold values from 1024 to 2048
Outputs:
- loss: float32 [], replicated
- logit_grad: float32 [16384, 4096], P('cell', 'spot')
- expr_grad: float32 [16384, 2048], P('cell', 'spot')
The draws below stay inside these ranges and needn't reach their ends.
All inputs are finite; a program needn't handle non-finite values.
Results may differ from the reference program's by a relative error of at most 0.0003.
Values sent between devices are 32-bit elements; how exact they have to be, the bound alone decides.
No kernel may reach another device: no remote copies, remote signals or barrier semaphores. Data moves between devices by JAX's collectives and lax.ppermute only.
A program may use at most 128 MiB of HBM per device.

```python
import jax
import jax.numpy as jnp
from jax import lax

GENES = 2048
SLIDES = 4
CELLS = 16384
SPOTS = 4096


def set_ends(values, key, low, high):
    spot = [jax.random.randint(jax.random.fold_in(key, axis), (), 0, length) for axis, length in enumerate(values.shape)]
    main_axis = values.shape.index(max(values.shape))
    neighbour = spot[:main_axis] + [(spot[main_axis] + 1) % values.shape[main_axis]] + spot[main_axis + 1:]
    return values.at[tuple(spot)].set(low).at[tuple(neighbour)].set(high)


def shard_levels(stream_key, extent, shards, low, high):
    gain, own = 1.0, jax.random.fold_in(stream_key, 6)
    for dim, parts in shards:
        heights = jnp.exp(jax.random.uniform(jax.random.fold_in(own, dim), (parts,), jnp.float32, low / len(shards), high / len(shards)))
        gain = gain * jnp.repeat(heights, extent[dim] // parts).reshape([-1 if axis == dim else 1 for axis in range(len(extent))])
    return gain


def centred(key, shape, width, reach, pieces=(), kind=jnp.bfloat16):
    array = jax.random.normal(key, shape, jnp.float32) * width
    if len(pieces) > 0:
        array = shard_levels(key, shape, pieces, -0.22, 0.18) * array
    return jnp.clip(array, min=-reach, max=reach).astype(kind)


def setup_inputs(seed: int = 0) -> dict:
    key_of = jax.random.split(jax.random.key(seed), 7)
    logits = centred(key_of[0], (CELLS, SPOTS), 2.0, 8.0, ((0, 8), (1, 4)), jnp.float32)
    expression = centred(key_of[1], (CELLS, GENES), 1.0, 6.0, ((0, 8),), jnp.float32)
    spatial = centred(key_of[2], (GENES, SPOTS), 1.0, 6.0, ((0, 8), (1, 4)), jnp.float32)
    masks = set_ends((jax.random.randint(key_of[3], (SLIDES, GENES), 0, 2) < 1).astype(jnp.int32), jax.random.fold_in(key_of[3], 1), 0, 1)
    slide_ids = set_ends(jax.random.randint(key_of[4], (SPOTS,), 0, SLIDES), jax.random.fold_in(key_of[4], 1), 0, SLIDES - 1).astype(jnp.int32)
    counts = set_ends(jax.random.randint(key_of[5], (SLIDES,), GENES // 2, GENES + 1), jax.random.fold_in(key_of[5], 1), GENES // 2, GENES).astype(jnp.int32)
    return dict(logits=logits, expression=expression, spatial=spatial, masks=masks, slide_ids=slide_ids, counts=counts)


@jax.custom_vjp
def low(v):
    return lax.optimization_barrier(v.astype(jnp.bfloat16)).astype(jnp.float32)

@jax.custom_vjp
def low_back(v):
    return v

def low_keep(v):
    return (low(v), None)

def low_pass(kept, grad):
    return (grad,)

def back_keep(v):
    return (v, None)

def back_low(kept, grad):
    return (low(grad),)
low.defvjp(low_keep, low_pass)
low_back.defvjp(back_keep, back_low)
eps = 1e-06

def objective(logits, expression, spatial, masks, slide_ids, counts):
    col_top = lax.optimization_barrier(jnp.max(logits, axis=0))
    exp_vals = jnp.exp(logits - col_top)
    mapping = exp_vals / lax.optimization_barrier(jnp.sum(exp_vals, axis=0))
    predicted = lax.dot_general(expression, mapping, (((0,), (0,)), ((), ())), precision=lax.Precision.HIGHEST)
    onehot = (slide_ids[None, :] == jnp.arange(SLIDES, dtype=jnp.int32)[:, None]).astype(jnp.float32)
    mask_f = masks.astype(jnp.float32)
    product = predicted * spatial
    squared = predicted * predicted
    spat_sq = spatial * spatial

    def by_slide(values):
        return lax.dot_general(onehot, values, (((1,), (1,)), ((), ())), precision=lax.Precision.HIGHEST)
    gene_cos = by_slide(product) / (jnp.sqrt(by_slide(squared) + eps) * jnp.sqrt(by_slide(spat_sq) + eps))
    weights = mask_f / counts.astype(jnp.float32)[:, None]
    gene_term = jnp.sum(weights * gene_cos) / SLIDES
    spot_mask = jnp.dot(mask_f.T, onehot, precision=lax.Precision.HIGHEST)
    first = lax.optimization_barrier(jnp.sum(spot_mask * product, axis=0))
    second = lax.optimization_barrier(jnp.sum(spot_mask * squared, axis=0))
    third = lax.optimization_barrier(jnp.sum(spot_mask * spat_sq, axis=0))
    spot_cos = first / (jnp.sqrt(second + eps) * jnp.sqrt(third + eps))
    spot_term = jnp.mean(spot_cos)
    mass = lax.optimization_barrier(jnp.mean(mapping, axis=1))
    density = -jnp.mean(jnp.log(CELLS * mass))
    return density - gene_term - spot_term

def reference(logits, expression, spatial, masks, slide_ids, counts):

    def closed(logit_in, expr_in):
        return objective(logit_in, expr_in, spatial, masks, slide_ids, counts)
    loss, pullback = jax.vjp(closed, logits, expression)
    grad_logits, grad_expr = pullback(jnp.ones_like(loss))
    scale = float(CELLS * SPOTS)
    return (loss, grad_logits * scale, grad_expr * scale)
```

```python
import functools

import jax
import jax.numpy as jnp
from jax import lax
from jax.experimental import pallas as pl
from jax.experimental.pallas import tpu as pltpu
from jax.sharding import PartitionSpec as P

eps = 1e-06
F32 = jnp.float32
BF16 = jnp.bfloat16
MIB = 1024 * 1024


def shape_of(*dims, dtype=F32):
    return jax.ShapeDtypeStruct(dims, dtype)


def params(mib):
    return pltpu.CompilerParams(vmem_limit_bytes=mib * MIB)


def split(v):
    high = v.astype(BF16)
    return high, (v - high.astype(F32)).astype(BF16)


def dot(a, b, ca, cb, precision=None):
    return lax.dot_general(
        a, b, (((ca,), (cb,)), ((), ())), precision=precision, preferred_element_type=F32
    )


def dot3(ah, al, bh, bl, ca, cb):
    return dot(ah, bh, ca, cb) + dot(al, bh, ca, cb) + dot(ah, bl, ca, cb)


def exact(a, b, ca, cb):
    return dot(a, b, ca, cb, lax.Precision.HIGHEST)


def cost(flops, nbytes):
    return pl.CostEstimate(flops=int(flops), bytes_accessed=int(nbytes), transcendentals=0)


def exp_body(logits, high, low, sums):
    vals = jnp.exp(logits[...])
    high[...], low[...] = split(vals)

    @pl.when(pl.program_id(0) == 0)
    def _():
        sums[...] = jnp.zeros_like(sums)

    sums[...] += jnp.sum(vals.reshape(-1, 8, vals.shape[1]), axis=0)


def exp_split(logits):
    rows, cols = logits.shape
    step = 256
    tile = pl.BlockSpec((step, cols), lambda i: (i, 0))
    return pl.pallas_call(
        exp_body,
        grid=(rows // step,),
        in_specs=[tile],
        out_specs=[tile, tile, pl.BlockSpec((8, cols), lambda i: (0, 0))],
        out_shape=[shape_of(rows, cols, dtype=BF16)] * 2 + [shape_of(8, cols)],
        compiler_params=params(32),
        cost_estimate=cost(rows * cols * 10, rows * cols * 8),
    )(logits)


def part_body(order, source, high, low):
    high[...], low[...] = split(source[...])


def part_split(expression, order, shard):
    rows, genes = expression.shape
    step = rows // 2
    if shard % 128:
        expression = expression.reshape(rows, -1, shard)[:, order].reshape(rows, genes)
        shard = genes // 8
        order = jnp.arange(8, dtype=jnp.int32)
    tile = pl.BlockSpec((step, shard), lambda p, i, order: (i, p))
    return pl.pallas_call(
        part_body,
        grid_spec=pltpu.PrefetchScalarGridSpec(
            num_scalar_prefetch=1,
            grid=(genes // shard, rows // step),
            in_specs=[pl.BlockSpec((step, shard), lambda p, i, order: (i, order[p]))],
            out_specs=[tile, tile],
        ),
        out_shape=[shape_of(rows, genes, dtype=BF16)] * 2,
        compiler_params=params(32),
        cost_estimate=cost(rows * genes * 4, rows * genes * 8),
    )(order, expression)


def send_body(eh, el, mh, ml, out):
    out[...] = dot3(eh[...], el[...], mh[...], ml[...], 0, 0)


def keep_body(half, eh, el, mh, ml, add, keep, send):
    vals = dot3(eh[...], el[...], mh[...], ml[...], 0, 0) + add[...]

    @pl.when(pl.program_id(0) < half)
    def _():
        keep[...] = vals

    @pl.when(pl.program_id(0) >= half)
    def _():
        send[...] = vals


def predict(eparts, mparts, unit, where, count, column, width, add=None):
    rows = mparts[0].shape[0]
    etile = pl.BlockSpec((rows, unit), lambda i: (0, where(i)))
    mtile = pl.BlockSpec((rows, width), lambda i: (0, column))
    flops = 6 * rows * unit * count * width
    traffic = 4 * rows * (unit * count + width) + 4 * unit * count * width
    if add is None:
        return pl.pallas_call(
            send_body,
            grid=(count,),
            in_specs=[etile, etile, mtile, mtile],
            out_specs=pl.BlockSpec((unit, width), lambda i: (i, 0)),
            out_shape=shape_of(unit * count, width),
            compiler_params=params(40),
            cost_estimate=cost(flops, traffic),
        )(*eparts, *mparts)
    half = count // 2
    return pl.pallas_call(
        functools.partial(keep_body, half),
        grid=(count,),
        in_specs=[etile, etile, mtile, mtile, pl.BlockSpec((unit, width), lambda i: (i, 0))],
        out_specs=[
            pl.BlockSpec((unit, width), lambda i: (jnp.minimum(i, half - 1), 0)),
            pl.BlockSpec((unit, width), lambda i: (jnp.maximum(i - half, 0), 0)),
        ],
        out_shape=[shape_of(unit * half, width)] * 2,
        compiler_params=params(40),
        cost_estimate=cost(flops, traffic),
    )(*eparts, *mparts, add)


def stats_body(kept, came, sums, spatial, mask, onehot, pred, spots, genes):
    total = jnp.sum(sums[...], axis=0, keepdims=True)
    vals = (kept[...] + came[...]) / total
    pred[...] = vals
    spat = spatial[...]
    seen = dot(mask[...].astype(BF16), onehot[...].astype(BF16), 0, 0)
    terms = (vals * spat, vals * vals, spat * spat)
    rows = [jnp.sum(seen * t, axis=0, keepdims=True) for t in terms]
    spots[...] = jnp.concatenate(rows + [jnp.zeros((5, rows[0].shape[1]), F32)], axis=0)
    genes[...] = jnp.concatenate([exact(onehot[...], t, 1, 1) for t in terms], axis=0)


def stats(kept, came, sums, spatial, mask, onehot, column):
    shard, width = kept.shape
    whole = pl.BlockSpec((shard, width), lambda i: (0, 0))
    strip = pl.BlockSpec((8, width), lambda i: (0, column))
    return pl.pallas_call(
        stats_body,
        grid=(1,),
        in_specs=[
            whole,
            whole,
            strip,
            pl.BlockSpec((shard, width), lambda i: (0, column)),
            pl.BlockSpec((8, shard), lambda i: (0, 0)),
            strip,
        ],
        out_specs=[
            whole,
            pl.BlockSpec((8, width), lambda i: (0, 0)),
            pl.BlockSpec((24, shard), lambda i: (0, 0)),
        ],
        out_shape=[shape_of(shard, width), shape_of(8, width), shape_of(24, shard)],
        compiler_params=params(32),
        cost_estimate=cost(shard * width * 40, shard * width * 16),
    )(kept, came, sums, spatial, mask, onehot)


def grad_body(slides, spots_total, parts, *refs):
    preds = refs[:parts]
    sums, spatial, mask, onehot, counts, gene_sums, spot_sums = refs[parts : parts + 7]
    outs = refs[parts + 7 : -2]
    inner, losses = refs[-2:]
    size = mask.shape[1]
    dot_g, pp_g, gg_g = (gene_sums[8 * i : 8 * i + 8, :] for i in range(3))
    norm_p, norm_s = jnp.sqrt(pp_g + eps), jnp.sqrt(gg_g + eps)
    weights = mask[...] / counts[...][:, :1]
    gene_part = jnp.sum(weights * (dot_g / (norm_p * norm_s))) / slides
    gene_weight = -weights / slides
    coef_s = gene_weight / (norm_p * norm_s)
    coef_p = gene_weight * dot_g / (norm_p * norm_p * norm_p * norm_s)
    a, b, c = (spot_sums[i : i + 1, :] for i in range(3))
    near_p, near_s = jnp.sqrt(b + eps), jnp.sqrt(c + eps)
    spot_part = jnp.sum(a / (near_p * near_s)) / spots_total
    edge_s = (-1.0 / spots_total) / (near_p * near_s)
    edge_p = (-1.0 / spots_total) * a / (near_p * near_p * near_p * near_s)
    total = jnp.sum(sums[...], axis=0, keepdims=True)
    hot = onehot[...]
    seen = dot(mask[...].astype(BF16), hot.astype(BF16), 0, 0)
    pred = jnp.concatenate([r[...] for r in preds], axis=1)
    grad = spatial[...] * (exact(coef_s, hot, 0, 0) + seen * edge_s) - pred * (
        exact(coef_p, hot, 0, 0) + seen * edge_p
    )
    row = jnp.sum(pred * grad, axis=0, keepdims=True)
    inner[...] = jnp.broadcast_to(row, inner.shape)
    grad = grad / total
    start = 0
    for out in outs:
        out[...] = grad[start : start + out.shape[0]]
        start += out.shape[0]
    lane = lax.broadcasted_iota(jnp.int32, losses.shape, 1)
    losses[...] = jnp.where(lane == 0, gene_part, jnp.where(lane == 1, spot_part, 0.0))


def gradient(preds, sums, spatial, mask, onehot, counts, gene_sums, spot_sums, heights, slides, spots_total):
    shard, cols = spatial.shape
    args = (*preds, sums, spatial, mask, onehot, counts, gene_sums, spot_sums)
    outs = [shape_of(h, cols) for h in heights] + [shape_of(8, cols), shape_of(8, 128)]
    return pl.pallas_call(
        functools.partial(grad_body, float(slides), float(spots_total), len(preds)),
        grid=(1,),
        in_specs=[pl.BlockSpec(a.shape, lambda i: (0, 0)) for a in args],
        out_specs=[pl.BlockSpec(o.shape, lambda i: (0, 0)) for o in outs],
        out_shape=outs,
        compiler_params=params(40),
        cost_estimate=cost(shard * cols * 60, shard * cols * 12),
    )(*args)


def mass_body(sums, mh, ml, out):
    inv = 1.0 / jnp.sum(sums[...], axis=0, keepdims=True)
    ih, il = split(jnp.broadcast_to(inv, (8, inv.shape[1])))
    out[...] = dot3(ih, il, mh[...], ml[...], 1, 1)


def mass_rows(sums, mparts):
    rows, cols = mparts[0].shape
    step = 512
    tile = pl.BlockSpec((step, cols), lambda i: (i, 0))
    return pl.pallas_call(
        mass_body,
        grid=(rows // step,),
        in_specs=[pl.BlockSpec((8, cols), lambda i: (0, 0)), tile, tile],
        out_specs=pl.BlockSpec((8, step), lambda i: (0, i)),
        out_shape=shape_of(8, rows),
        compiler_params=params(32),
        cost_estimate=cost(rows * cols * 48, rows * cols * 4),
    )(sums, *mparts)


def pull_body(dens, sums, mh, ml, out):
    dh, dl = split(jnp.broadcast_to(dens[...][:1], dens.shape))

    @pl.when(pl.program_id(0) == 0)
    def _():
        out[...] = jnp.zeros_like(out)

    out[...] += dot3(dh, dl, mh[...], ml[...], 1, 0) / jnp.sum(sums[...], axis=0, keepdims=True)


def pull_cols(dens, sums, mparts):
    rows, cols = mparts[0].shape
    step = 512
    tile = pl.BlockSpec((step, cols), lambda i: (i, 0))
    strip = pl.BlockSpec((8, cols), lambda i: (0, 0))
    return pl.pallas_call(
        pull_body,
        grid=(rows // step,),
        in_specs=[pl.BlockSpec((8, step), lambda i: (0, i)), strip, tile, tile],
        out_specs=strip,
        out_shape=shape_of(8, cols),
        compiler_params=params(32),
        cost_estimate=cost(rows * cols * 48, rows * cols * 4),
    )(dens, sums, *mparts)


def expr_body(number, height, half, ids, near, far, across, mh, ml, ph, pls, *refs):
    outs, (oh, ol, ch, cl) = refs[:-4], refs[-4:]

    @pl.when(pl.program_id(0) == 0)
    def _():
        for n in range(number):
            at = ids[n]
            inside = pl.ds(pl.multiple_of((at % half) * height, 16), height)
            own = jnp.where(at < half, near[inside, :], far[inside, :])
            other = across[pl.ds(pl.multiple_of(ids[number + n] * height, 16), height), :]
            put = slice(n * height, (n + 1) * height)
            oh[put, :], ol[put, :] = split(own)
            ch[put, :], cl[put, :] = split(other)

    vals = dot3(mh[...], ml[...], oh[...], ol[...], 1, 1) + dot3(
        ph[...], pls[...], ch[...], cl[...], 1, 1
    )
    width = vals.shape[1] // len(outs)
    for n, out in enumerate(outs):
        out[...] = vals[:, n * width : (n + 1) * width]


def expr_part(ids, near, far, across, mparts, pparts, height, blocks, number):
    rows, cols = mparts[0].shape
    step = 512
    half = near.shape[0] // height
    tile = pl.BlockSpec((step, cols), lambda i, ids: (i, 0))
    width = number * height // blocks
    return pl.pallas_call(
        functools.partial(expr_body, number, height, half),
        grid_spec=pltpu.PrefetchScalarGridSpec(
            num_scalar_prefetch=1,
            grid=(rows // step,),
            in_specs=[pl.BlockSpec(a.shape, lambda i, ids: (0, 0)) for a in (near, far, across)]
            + [tile] * 4,
            out_specs=[pl.BlockSpec((step, width), lambda i, ids: (i, 0))] * blocks,
            scratch_shapes=[pltpu.VMEM((number * height, cols), BF16)] * 4,
        ),
        out_shape=[shape_of(rows, width)] * blocks,
        compiler_params=params(48),
        cost_estimate=cost(12 * rows * cols * number * height, rows * cols * 8),
    )(ids, near, far, across, *mparts, *pparts)


def logit_body(pieces, heights, scale, dens, sums, inner, eh, el, mh, ml, *refs):
    grads, (out, dh, dl) = refs[:-3], refs[-3:]

    @pl.when(pl.program_id(0) == 0)
    def _():
        at = 0
        for p in range(pieces):
            for q, height in enumerate(heights):
                source = grads[2 * q + (p >= pieces // 2)]
                inside = p % (pieces // 2)
                dh[at : at + height, :], dl[at : at + height, :] = split(
                    source[inside * height : (inside + 1) * height, :]
                )
                at += height

    inv = 1.0 / jnp.sum(sums[...], axis=0, keepdims=True)
    column = jnp.transpose(dens[...])[:, :1]
    vals = dot3(eh[...], el[...], dh[...], dl[...], 1, 0) + (column - inner[...][:1]) * inv
    out[...] = (mh[...].astype(F32) + ml[...].astype(F32)) * vals * scale


def logit_part(dens, sums, inner, eparts, mparts, grads, heights, pieces, scale):
    rows, cols = mparts[0].shape
    genes = eparts[0].shape[1]
    step = 256
    strip = pl.BlockSpec((8, cols), lambda i: (0, 0))
    tile = pl.BlockSpec((step, cols), lambda i: (i, 0))
    return pl.pallas_call(
        functools.partial(logit_body, pieces, heights, scale),
        grid=(rows // step,),
        in_specs=[pl.BlockSpec((8, step), lambda i: (0, i)), strip, strip]
        + [pl.BlockSpec((step, genes), lambda i: (i, 0))] * 2
        + [tile] * 2
        + [pl.BlockSpec(g.shape, lambda i: (0, 0), pipeline_mode=pl.Buffered(1)) for g in grads],
        out_specs=tile,
        out_shape=shape_of(rows, cols),
        scratch_shapes=[pltpu.VMEM((genes, cols), BF16)] * 2,
        compiler_params=params(52),
        cost_estimate=cost(6 * rows * cols * genes, rows * genes * 4 + rows * cols * 8),
    )(dens, sums, inner, *eparts, *mparts, *grads)


def join_body(shards, heights, scale, *refs):
    out = refs[-1]
    shard = sum(heights)
    at = 0
    for q, height in enumerate(heights):
        vals = (refs[2 * q][...] + refs[2 * q + 1][...]) * scale
        for b in range(shards):
            out[:, b * shard + at : b * shard + at + height] = vals[:, b * height : (b + 1) * height]
        at += height


def join(pairs, heights, shards, scale):
    flat = [v for pair in pairs for v in pair]
    rows = flat[0].shape[0]
    step = 512
    genes = shards * sum(heights)
    return pl.pallas_call(
        functools.partial(join_body, shards, heights, scale),
        grid=(rows // step,),
        in_specs=[pl.BlockSpec((step, v.shape[1]), lambda i: (i, 0)) for v in flat],
        out_specs=pl.BlockSpec((step, genes), lambda i: (i, 0)),
        out_shape=shape_of(rows, genes),
        compiler_params=params(32),
        cost_estimate=cost(rows * genes * 2, rows * genes * 12),
    )(*flat)


def swap(v, axis, bit):
    size = lax.axis_size(axis)
    return lax.ppermute(v, axis, [(i, i ^ (1 << bit)) for i in range(size)])


def add_all(v, axis):
    for bit in range(lax.axis_size(axis).bit_length() - 1):
        v = v + swap(v, axis, bit)
    return v


def reverse(value, bits):
    return sum(((value >> b) & 1) << (bits - 1 - b) for b in range(bits))


def on_device(logits, expression, spatial, masks, slide_ids, counts):
    cells, spots_n = lax.axis_size("cell"), lax.axis_size("spot")
    me, mine = lax.axis_index("cell"), lax.axis_index("spot")
    rows, cols = logits.shape
    shard = spatial.shape[0]
    slides, genes = masks.shape
    cells_total, spots_total = rows * cells, cols * spots_n
    cell_bits = cells.bit_length() - 1
    per_block = cells // spots_n
    block_bits = per_block.bit_length() - 1
    scale = float(cells_total * spots_total)

    other_logits = swap(logits, "spot", 0)
    *mparts, sums = exp_split(logits)
    order = me ^ reverse(jnp.arange(cells, dtype=jnp.int32), cell_bits)
    eparts = part_split(expression, order, shard)
    sums = add_all(sums, "cell")

    mask8 = jnp.pad(masks.astype(F32), ((0, 8 - slides), (0, 0)))
    mask8 = lax.dynamic_slice_in_dim(mask8, me * shard, shard, 1)
    onehot = (slide_ids[None, :] == jnp.arange(8, dtype=jnp.int32)[:, None]).astype(F32)
    counts8 = jnp.broadcast_to(
        jnp.pad(counts.astype(F32), (0, 8 - slides), constant_values=1.0)[:, None], (8, 128)
    )

    unit = 256
    count = genes // 2 // unit
    width = 256
    preds, spot_stats, gene_stats = [], [], 0.0
    for q in range(cols // width):
        z_first = cells == 8 and shard == unit and q == 1
        if z_first:
            bits = (1, 0, 2)
            send_at = lambda i: (i // 2) * 4 + 2 + i % 2
            keep_at = lambda i: (i // 2) * 4 + i % 2
        else:
            bits = tuple(range(cell_bits))
            send_at = lambda i: count + i
            keep_at = lambda i: i
        send = predict(eparts, mparts, unit, send_at, count, q, width)
        came = swap(send, "cell", bits[0])
        kept, send = predict(eparts, mparts, unit, keep_at, count, q, width, came)
        for bit in bits[1:-1]:
            both = kept, swap(send, "cell", bit)
            half = kept.shape[0] // 2
            send = both[0][half:] + both[1][half:]
            kept = both[0][:half] + both[1][:half]
        came = swap(send, "cell", bits[-1])
        pred, spot_q, gene_q = stats(kept, came, sums, spatial, mask8, onehot, q)
        preds.append(pred)
        spot_stats.append(spot_q)
        gene_stats = gene_stats + gene_q
    spot_stats = add_all(jnp.concatenate(spot_stats, axis=1), "cell")
    mass = mass_rows(sums, mparts)[:1].reshape(-1, shard)
    joint = add_all(jnp.concatenate([gene_stats, mass], axis=0), "spot")
    gene_stats = joint[:24]
    mass = joint[24:].reshape(1, rows) / spots_total
    density_part = -jnp.sum(jnp.log(cells_total * mass)) / cells_total
    dens = jnp.broadcast_to(-1.0 / (cells_total * spots_total * mass), (8, rows))

    heights = (shard // 4,) * 4
    *grads, inner, losses = gradient(
        preds, sums, spatial, mask8, onehot, counts8, gene_stats, spot_stats, heights, slides, spots_total
    )

    pparts = exp_split(other_logits)[:2]
    inner = inner + pull_cols(dens, sums, mparts)
    first = jnp.broadcast_to(density_part - losses[0, 0], (8, 128))
    tail = add_all(jnp.concatenate([inner, first], axis=1), "cell")
    inner = tail[:, :cols]
    loss = tail[0, cols] - add_all(jnp.broadcast_to(losses[0, 1], (8, 128)), "spot")[0, 0]

    blocks = spots_n // 2
    far_w = jnp.arange(blocks, dtype=jnp.int32)[:, None] << 1
    wanted = ((mine ^ far_w) * per_block + jnp.arange(per_block, dtype=jnp.int32)[None, :]) ^ me
    wanted = wanted.reshape(-1)
    place = reverse(wanted, cell_bits)
    low_bits = cell_bits - block_bits - 1
    short = ((place >> (low_bits + 1)) << low_bits) | (place & ((1 << low_bits) - 1))
    ids = jnp.concatenate([place, short]).astype(jnp.int32)
    core_bit = ((me >> block_bits) ^ mine) & 1

    gathered, pairs = [], []
    for q, height in enumerate(heights):
        near = grads[q]
        for bit in range(cell_bits - 1, 0, -1):
            near = jnp.concatenate([near, swap(near, "cell", bit)], axis=0)
        far = swap(near, "cell", 0)
        gathered += [near, far]

        def part(v):
            v = v.reshape(1 << (block_bits - 1), 2, 1 << low_bits, height, cols)
            return lax.dynamic_index_in_dim(v, 1 - core_bit, 1, keepdims=False).reshape(-1, cols)

        across = swap(jnp.concatenate([part(near), part(far)], axis=0), "spot", 0)
        outs = expr_part(ids, near, far, across, mparts, pparts, height, blocks, wanted.size)
        outs = list(outs)
        bit = spots_n.bit_length() - 2
        while len(outs) > 2:
            half = len(outs) // 2
            came = swap(jnp.concatenate(outs[half:], axis=1), "spot", bit)
            came = jnp.split(came, half, axis=1)
            outs = [a + b for a, b in zip(outs[:half], came)]
            bit -= 1
        pairs.append((outs[0], swap(outs[1], "spot", bit)))

    logit_grad = logit_part(dens, sums, inner, eparts, mparts, gathered, heights, cells, scale)
    expr_grad = join(pairs, heights, per_block, scale)
    return (loss, logit_grad, expr_grad)


def solution(mesh):
    placed = (P("cell", "spot"), P("cell", None), P("cell", "spot"), P(), P("spot"), P())
    return jax.shard_map(
        on_device,
        mesh=mesh,
        in_specs=placed,
        out_specs=(P(), P("cell", "spot"), P("cell", "spot")),
        check_vma=False,
    )
```

```python
import functools

import jax
import jax.numpy as jnp
from jax import lax
from jax.experimental import pallas as pl
from jax.experimental.pallas import tpu as pltpu
from jax.sharding import PartitionSpec as P

eps = 1e-06
F32 = jnp.float32
BF16 = jnp.bfloat16
MIB = 1024 * 1024


def shape_of(*dims, dtype=F32):
    return jax.ShapeDtypeStruct(dims, dtype)


def hbm(*dims):
    return pltpu.HBM(dims[:-1], dims[-1])


def after(value, *others):
    return lax.optimization_barrier((value, *others))[0]


def params(mib):
    return pltpu.CompilerParams(vmem_limit_bytes=mib * MIB)


def split(v):
    high = v.astype(BF16)
    return high, (v - high.astype(F32)).astype(BF16)


def dot(a, b, ca, cb, precision=None):
    return lax.dot_general(
        a, b, (((ca,), (cb,)), ((), ())), precision=precision, preferred_element_type=F32
    )


def dot3(ah, al, bh, bl, ca, cb):
    return dot(ah, bh, ca, cb) + dot(al, bh, ca, cb) + dot(ah, bl, ca, cb)


def exact(a, b, ca, cb):
    return dot(a, b, ca, cb, lax.Precision.HIGHEST)


def cost(flops, nbytes):
    return pl.CostEstimate(flops=0, bytes_accessed=0, transcendentals=0)


def simple(body, outs, *args, prefetch=None):
    def spec(v):
        return pl.BlockSpec(v.shape, lambda i, *_: (0,) * len(v.shape))

    number = 0 if prefetch is None else 1
    return pl.pallas_call(
        body,
        grid_spec=pltpu.PrefetchScalarGridSpec(
            num_scalar_prefetch=number,
            grid=(1,),
            in_specs=[spec(a) for a in args],
            out_specs=[spec(o) for o in outs],
        ),
        out_shape=list(outs),
        compiler_params=params(32),
        cost_estimate=cost(0, 0),
    )(*([] if prefetch is None else [prefetch]), *args)


def add_body(a, b, out):
    out[...] = a[...] + b[...]


def add(a, b):
    return simple(add_body, [shape_of(*a.shape)], a, b)[0]


def add_split_body(kept, came, low, high):
    if len(kept.shape) == 3:
        low[...], high[...] = kept[0] + came[0], kept[1] + came[1]
    else:
        half = kept.shape[1] // 2
        low[...] = kept[:, :half] + came[:, :half]
        high[...] = kept[:, half:] + came[:, half:]


def add_split(kept, came):
    rows, cols = kept.shape[-2:]
    out = shape_of(rows, cols if kept.ndim == 3 else cols // 2)
    return simple(add_split_body, [out, out], kept, came)


def glue_body(*refs):
    *sources, out = refs
    at = 0
    for source in sources:
        out[at : at + source.shape[0], :] = source[...]
        at += source.shape[0]


def glue(*parts):
    return simple(glue_body, [shape_of(sum(p.shape[0] for p in parts), parts[0].shape[1])], *parts)[0]


def pick_body(outer, size, which, *refs):
    *sources, out = refs
    at = 0
    for source in sources:
        for n in range(outer):
            start = pl.multiple_of((2 * n + which[0]) * size, 8)
            out[at : at + size, :] = source[pl.ds(start, size), :]
            at += size


def pick(which, outer, size, *sources):
    out = shape_of(outer * size * len(sources), sources[0].shape[1])
    body = functools.partial(pick_body, outer, size)
    return simple(body, [out], *sources, prefetch=which)[0]


def exp_body(with_sums, logits, high, low, *sums):
    vals = jnp.exp(logits[...])
    high[...], low[...] = split(vals)
    if with_sums:

        @pl.when(pl.program_id(0) == 0)
        def _():
            sums[0][...] = jnp.zeros_like(sums[0])

        sums[0][...] += jnp.sum(vals.reshape(-1, 8, vals.shape[1]), axis=0)


def exp_split(logits, with_sums):
    rows, cols = logits.shape
    step = 1024
    tile = pl.BlockSpec((step, cols), lambda i: (i, 0))
    outs, shapes = [tile, tile], [hbm(rows, cols, BF16)] * 2
    if with_sums:
        outs += [pl.BlockSpec((8, cols), lambda i: (0, 0))]
        shapes += [shape_of(8, cols)]
    return pl.pallas_call(
        functools.partial(exp_body, with_sums),
        grid=(rows // step,),
        in_specs=[tile],
        out_specs=outs,
        out_shape=shapes,
        compiler_params=params(56),
        cost_estimate=cost(rows * cols * 10, rows * cols * 8),
    )(logits)


def mass_body(sums, mh, ml, out):
    inv = 1.0 / jnp.sum(sums[...], axis=0, keepdims=True)
    ih, il = split(jnp.broadcast_to(inv, (8, inv.shape[1])))
    out[...] = dot3(ih, il, mh[...], ml[...], 1, 1)


def mass_rows(sums, mparts):
    rows, cols = mparts[0].shape
    step = 512
    tile = pl.BlockSpec((step, cols), lambda i: (i, 0))
    return pl.pallas_call(
        mass_body,
        grid=(rows // step,),
        in_specs=[pl.BlockSpec((8, cols), lambda i: (0, 0)), tile, tile],
        out_specs=pl.BlockSpec((8, step), lambda i: (0, i)),
        out_shape=shape_of(8, rows),
        compiler_params=params(56),
        cost_estimate=cost(rows * cols * 48, rows * cols * 4),
    )(sums, *mparts)


def turn(logits, th, tl):
    @pl.when(pl.program_id(0) == 0)
    def _():
        th[...], tl[...] = split(jnp.transpose(jnp.exp(logits[...])))


def send_body(order, logits, source, out, th, tl):
    turn(logits, th, tl)
    out[...] = dot3(th[...], tl[...], *split(source[...]), 1, 0)


def keep_body(order, th, tl, source, out):
    out[...] = dot3(th[...], tl[...], *split(source[...]), 1, 0)


def both_body(across, order, logits, near, far, keep, send, th, tl):
    turn(logits, th, tl)
    first = dot3(th[...], tl[...], *split(near[...]), 1, 0)
    second = dot3(th[...], tl[...], *split(far[...]), 1, 0)
    if not across:
        keep[...], send[...] = first, second
        return
    number = pl.num_programs(0) // 2

    @pl.when(pl.program_id(0) < number)
    def _():
        keep[0], keep[1] = first, second

    @pl.when(pl.program_id(0) >= number)
    def _():
        send[0], send[1] = first, second


def predict(kind, order, expression, unit, column, width, logits, turned=None):
    rows, genes = expression.shape
    count = genes // 2 // unit
    near = pl.BlockSpec((rows, unit), lambda i, order: (0, order[i]))
    far = pl.BlockSpec((rows, unit), lambda i, order: (0, order[count + i]))
    piece = pl.BlockSpec((rows, width), lambda i, order: (0, column))
    flipped = pl.BlockSpec((width, rows), lambda i, order: (0, 0))
    block = pl.BlockSpec((width, unit), lambda i, order: (0, i))
    half = shape_of(width, genes // 2)
    scratch = []
    if kind == "send":
        body, args, ins = send_body, (logits, expression), [piece, far]
        outs, shapes = [block, flipped, flipped], [half] + [hbm(width, rows, BF16)] * 2
    elif kind == "keep":
        body, args, ins = keep_body, (*turned, expression), [flipped, flipped, near]
        outs, shapes = block, half
    else:
        body, args = functools.partial(both_body, kind == "across"), (logits, expression, expression)
        ins, scratch = [piece, near, far], [pltpu.VMEM((width, rows), BF16)] * 2
        outs, shapes = [block, block], [half, half]
        if kind == "across":
            mid = count // 2
            shapes = [shape_of(2, width, genes // 4)] * 2
            outs = [
                pl.BlockSpec((2, width, unit), lambda i, order: (0, 0, jnp.minimum(i, mid - 1))),
                pl.BlockSpec((2, width, unit), lambda i, order: (0, 0, jnp.maximum(i - mid, 0))),
            ]
    return pl.pallas_call(
        body,
        grid_spec=pltpu.PrefetchScalarGridSpec(
            num_scalar_prefetch=1, grid=(count,), in_specs=ins, out_specs=outs, scratch_shapes=scratch
        ),
        out_shape=shapes,
        compiler_params=params(56),
        cost_estimate=cost(3 * rows * genes * width, rows * genes * 4),
    )(order, *args)


def stats_body(turn, kept, came, sums, spatial, mask, onehot, pred, spots, genes):
    total = jnp.sum(sums[...], axis=0, keepdims=True)
    vals = kept[...] + came[...]
    if turn:
        vals = jnp.transpose(vals)
    vals = vals / total
    pred[...] = vals
    spat = spatial[...]
    seen = dot(mask[...].astype(BF16), onehot[...].astype(BF16), 0, 0)
    terms = (vals * spat, vals * vals, spat * spat)
    rows = [jnp.sum(seen * t, axis=0, keepdims=True) for t in terms]
    spots[...] = jnp.concatenate(rows + [jnp.zeros((5, rows[0].shape[1]), F32)], axis=0)
    genes[...] = jnp.concatenate([exact(onehot[...], t, 1, 1) for t in terms], axis=0)


def stats(kept, came, sums, spatial, mask, onehot, column):
    width, shard = kept.shape
    turn = shard % 128 == 0
    if not turn:
        kept, came = kept.T, came.T
    whole = pl.BlockSpec((shard, width), lambda i: (0, 0))
    given = pl.BlockSpec(kept.shape, lambda i: (0, 0))
    strip = pl.BlockSpec((8, width), lambda i: (0, column))
    return pl.pallas_call(
        functools.partial(stats_body, turn),
        grid=(1,),
        in_specs=[
            given,
            given,
            strip,
            pl.BlockSpec((shard, width), lambda i: (0, column)),
            pl.BlockSpec((8, shard), lambda i: (0, 0)),
            strip,
        ],
        out_specs=[
            whole,
            pl.BlockSpec((8, width), lambda i: (0, 0)),
            pl.BlockSpec((24, shard), lambda i: (0, 0)),
        ],
        out_shape=[shape_of(shard, width), shape_of(8, width), shape_of(24, shard)],
        compiler_params=params(32),
        cost_estimate=cost(shard * width * 40, shard * width * 16),
    )(kept, came, sums, spatial, mask, onehot)


def grad_body(slides, spots_total, parts, *refs):
    preds = refs[:parts]
    sums, spatial, mask, onehot, counts, gene_sums, spot_sums = refs[parts : parts + 7]
    outs = refs[parts + 7 : -2]
    inner, losses = refs[-2:]
    size = mask.shape[1]
    dot_g, pp_g, gg_g = (gene_sums[8 * i : 8 * i + 8, :] for i in range(3))
    norm_p, norm_s = jnp.sqrt(pp_g + eps), jnp.sqrt(gg_g + eps)
    weights = mask[...] / counts[...][:, :1]
    gene_part = jnp.sum(weights * (dot_g / (norm_p * norm_s))) / slides
    gene_weight = -weights / slides
    coef_s = gene_weight / (norm_p * norm_s)
    coef_p = gene_weight * dot_g / (norm_p * norm_p * norm_p * norm_s)
    a, b, c = (spot_sums[i : i + 1, :] for i in range(3))
    near_p, near_s = jnp.sqrt(b + eps), jnp.sqrt(c + eps)
    spot_part = jnp.sum(a / (near_p * near_s)) / spots_total
    edge_s = (-1.0 / spots_total) / (near_p * near_s)
    edge_p = (-1.0 / spots_total) * a / (near_p * near_p * near_p * near_s)
    total = jnp.sum(sums[...], axis=0, keepdims=True)
    hot = onehot[...]
    seen = dot(mask[...].astype(BF16), hot.astype(BF16), 0, 0)
    pred = jnp.concatenate([r[...] for r in preds], axis=1)
    grad = spatial[...] * (exact(coef_s, hot, 0, 0) + seen * edge_s) - pred * (
        exact(coef_p, hot, 0, 0) + seen * edge_p
    )
    row = jnp.sum(pred * grad, axis=0, keepdims=True)
    inner[...] = jnp.broadcast_to(row, inner.shape)
    grad = grad / total
    start = 0
    for out in outs:
        out[...] = grad[start : start + out.shape[0]]
        start += out.shape[0]
    lane = lax.broadcasted_iota(jnp.int32, losses.shape, 1)
    losses[...] = jnp.where(lane == 0, gene_part, jnp.where(lane == 1, spot_part, 0.0))


def gradient(preds, sums, spatial, mask, onehot, counts, gene_sums, spot_sums, heights, slides, spots_total):
    shard, cols = spatial.shape
    args = (*preds, sums, spatial, mask, onehot, counts, gene_sums, spot_sums)
    outs = [shape_of(h, cols) for h in heights] + [shape_of(8, cols), shape_of(8, 128)]
    return pl.pallas_call(
        functools.partial(grad_body, float(slides), float(spots_total), len(preds)),
        grid=(1,),
        in_specs=[pl.BlockSpec(a.shape, lambda i: (0, 0)) for a in args],
        out_specs=[pl.BlockSpec(o.shape, lambda i: (0, 0)) for o in outs],
        out_shape=outs,
        compiler_params=params(40),
        cost_estimate=cost(shard * cols * 60, shard * cols * 12),
    )(*args)


def pull_body(dens, sums, mh, ml, out):
    dh, dl = split(jnp.broadcast_to(dens[...][:1], dens.shape))

    @pl.when(pl.program_id(0) == 0)
    def _():
        out[...] = jnp.zeros_like(out)

    out[...] += dot3(dh, dl, mh[...], ml[...], 1, 0) / jnp.sum(sums[...], axis=0, keepdims=True)


def pull_cols(dens, sums, mparts):
    rows, cols = mparts[0].shape
    step = 512
    tile = pl.BlockSpec((step, cols), lambda i: (i, 0))
    strip = pl.BlockSpec((8, cols), lambda i: (0, 0))
    return pl.pallas_call(
        pull_body,
        grid=(rows // step,),
        in_specs=[pl.BlockSpec((8, step), lambda i: (0, i)), strip, tile, tile],
        out_specs=strip,
        out_shape=shape_of(8, cols),
        compiler_params=params(56),
        cost_estimate=cost(rows * cols * 48, rows * cols * 4),
    )(dens, sums, *mparts)


def expr_body(number, height, half, ids, near, far, across, mh, ml, ph, pls, *refs):
    outs, (oh, ol, ch, cl) = refs[:-4], refs[-4:]

    @pl.when(pl.program_id(0) == 0)
    def _():
        for n in range(number):
            at = ids[n]
            inside = pl.ds(pl.multiple_of((at % half) * height, 16), height)
            own = jnp.where(at < half, near[inside, :], far[inside, :])
            other = across[pl.ds(pl.multiple_of(ids[number + n] * height, 16), height), :]
            put = slice(n * height, (n + 1) * height)
            oh[put, :], ol[put, :] = split(own)
            ch[put, :], cl[put, :] = split(other)

    vals = dot3(mh[...], ml[...], oh[...], ol[...], 1, 1) + dot3(
        ph[...], pls[...], ch[...], cl[...], 1, 1
    )
    width = vals.shape[1] // len(outs)
    for n, out in enumerate(outs):
        out[...] = vals[:, n * width : (n + 1) * width]


def expr_part(ids, near, far, across, mparts, pparts, height, blocks, number):
    rows, cols = mparts[0].shape
    step = 512
    half = near.shape[0] // height
    tile = pl.BlockSpec((step, cols), lambda i, ids: (i, 0))
    width = number * height // blocks
    return pl.pallas_call(
        functools.partial(expr_body, number, height, half),
        grid_spec=pltpu.PrefetchScalarGridSpec(
            num_scalar_prefetch=1,
            grid=(rows // step,),
            in_specs=[pl.BlockSpec(a.shape, lambda i, ids: (0, 0)) for a in (near, far, across)]
            + [tile] * 4,
            out_specs=[pl.BlockSpec((step, width), lambda i, ids: (i, 0))] * blocks,
            scratch_shapes=[pltpu.VMEM((number * height, cols), BF16)] * 4,
        ),
        out_shape=[shape_of(rows, width)] * blocks,
        compiler_params=params(48),
        cost_estimate=cost(12 * rows * cols * number * height, rows * cols * 8),
    )(ids, near, far, across, *mparts, *pparts)


def logit_body(pieces, heights, unit, scale, order, dens, sums, inner, source, mh, ml, *refs):
    grads, (out, dh, dl) = refs[:-3], refs[-3:]

    @pl.when(pl.program_id(0) == 0)
    def _():
        shard = sum(heights)
        for p in range(pieces):
            base = order[p * shard // unit] * unit + p * shard % unit
            at = 0
            for q, height in enumerate(heights):
                grad = grads[2 * q + (p >= pieces // 2)]
                inside = p % (pieces // 2)
                rows = pl.ds(pl.multiple_of(base + at, 16), height)
                dh[rows, :], dl[rows, :] = split(grad[inside * height : (inside + 1) * height, :])
                at += height

    inv = 1.0 / jnp.sum(sums[...], axis=0, keepdims=True)
    column = jnp.transpose(dens[...])[:, :1]
    vals = dot3(*split(source[...]), dh[...], dl[...], 1, 0) + (column - inner[...][:1]) * inv
    out[...] = (mh[...].astype(F32) + ml[...].astype(F32)) * vals * scale


def logit_part(order, dens, sums, inner, expression, mparts, grads, heights, pieces, unit, scale):
    rows, cols = mparts[0].shape
    genes = expression.shape[1]
    step = 256
    strip = pl.BlockSpec((8, cols), lambda i, order: (0, 0))
    tile = pl.BlockSpec((step, cols), lambda i, order: (i, 0))
    return pl.pallas_call(
        functools.partial(logit_body, pieces, heights, unit, scale),
        grid_spec=pltpu.PrefetchScalarGridSpec(
            num_scalar_prefetch=1,
            grid=(rows // step,),
            in_specs=[pl.BlockSpec((8, step), lambda i, order: (0, i)), strip, strip]
            + [pl.BlockSpec((step, genes), lambda i, order: (i, 0))]
            + [tile] * 2
            + [
                pl.BlockSpec(g.shape, lambda i, order: (0, 0), pipeline_mode=pl.Buffered(1))
                for g in grads
            ],
            out_specs=tile,
            scratch_shapes=[pltpu.VMEM((genes, cols), BF16)] * 2,
        ),
        out_shape=shape_of(rows, cols),
        compiler_params=params(56),
        cost_estimate=cost(6 * rows * cols * genes, rows * genes * 4 + rows * cols * 8),
    )(order, dens, sums, inner, expression, *mparts, *grads)


def join_body(shards, heights, scale, *refs):
    out = refs[-1]
    shard = sum(heights)
    at = 0
    for q, height in enumerate(heights):
        vals = (refs[2 * q][...] + refs[2 * q + 1][...]) * scale
        for b in range(shards):
            out[:, b * shard + at : b * shard + at + height] = vals[:, b * height : (b + 1) * height]
        at += height


def join(pairs, heights, shards, scale):
    flat = [v for pair in pairs for v in pair]
    rows = flat[0].shape[0]
    step = 512
    genes = shards * sum(heights)
    return pl.pallas_call(
        functools.partial(join_body, shards, heights, scale),
        grid=(rows // step,),
        in_specs=[pl.BlockSpec((step, v.shape[1]), lambda i: (i, 0)) for v in flat],
        out_specs=pl.BlockSpec((step, genes), lambda i: (i, 0)),
        out_shape=shape_of(rows, genes),
        compiler_params=params(32),
        cost_estimate=cost(rows * genes * 2, rows * genes * 12),
    )(*flat)


class Line:
    def __init__(self):
        self.held = []

    def __call__(self, value):
        return after(value, *self.held) if self.held else value

    def mark(self, value):
        self.held = [value]

    def also(self, value):
        self.held = self.held + [value]


class Total:
    def __init__(self, line, value, axis, bits):
        self.line, self.value, self.axis, self.bits = line, value, axis, list(bits)
        self.come = swap(value, axis, self.bits.pop(0))

    def next(self):
        self.value = add(self.value, self.line(self.come))
        self.line.mark(self.value)
        self.come = swap(self.value, self.axis, self.bits.pop(0)) if self.bits else None

    def end(self):
        while self.come is not None:
            self.next()
        return self.value


def swap(v, axis, bit):
    size = lax.axis_size(axis)
    return lax.ppermute(v, axis, [(i, i ^ (1 << bit)) for i in range(size)])


def add_all(v, axis):
    for bit in range(lax.axis_size(axis).bit_length() - 1):
        v = add(v, swap(v, axis, bit))
    return v


def reverse(value, bits):
    return sum(((value >> b) & 1) << (bits - 1 - b) for b in range(bits))


def on_device(logits, expression, spatial, masks, slide_ids, counts):
    cells, spots_n = lax.axis_size("cell"), lax.axis_size("spot")
    me, mine = lax.axis_index("cell"), lax.axis_index("spot")
    rows, cols = logits.shape
    shard = spatial.shape[0]
    slides, genes = masks.shape
    cells_total, spots_total = rows * cells, cols * spots_n
    cell_bits = cells.bit_length() - 1
    per_block = cells // spots_n
    block_bits = per_block.bit_length() - 1
    scale = float(cells_total * spots_total)

    other_logits = swap(logits, "spot", 0)
    order = me ^ reverse(jnp.arange(cells, dtype=jnp.int32), cell_bits)
    unit = 256
    source = expression
    if shard != unit:
        source = source.reshape(rows, cells, shard)[:, order].reshape(rows, genes)
        order = jnp.arange(genes // unit, dtype=jnp.int32)

    mask8 = jnp.pad(masks.astype(F32), ((0, 8 - slides), (0, 0)))
    mask8 = lax.dynamic_slice_in_dim(mask8, me * shard, shard, 1)
    onehot = (slide_ids[None, :] == jnp.arange(8, dtype=jnp.int32)[:, None]).astype(F32)
    counts8 = jnp.broadcast_to(
        jnp.pad(counts.astype(F32), (0, 8 - slides), constant_values=1.0)[:, None], (8, 128)
    )

    line = Line()

    width = 256
    number = cols // width
    generic = not (cells == 8 and shard == unit and number == 4)
    cross = -1 if generic else 1
    keeps, sends, steps, found, turned, parts = {}, {}, {}, {}, {}, {}

    def make(kind, q):
        given = turned.get(q)
        if kind == "keep":
            given = line(given[0]), given[1]
        outs = predict(kind, order, source, unit, q, width, line(logits), given)
        if kind == "send":
            sends[q], *turned[q] = outs
        elif kind == "keep":
            keeps[q] = outs
        else:
            keeps[q], sends[q] = outs
        line.mark(keeps.get(q, sends.get(q)))
        if kind != "keep":
            found[q] = swap(sends[q], "cell", 1 if q == cross else 0)

    def step(q):
        bits = (1, 0, 2) if q == cross else tuple(range(cell_bits))
        at = steps.get(q, 0)
        steps[q] = at + 1
        if at < cell_bits - 1:
            kept, came = keeps[q], line(found[q])
            kept, out = add_split(kept, came)
            line.mark(out)
            keeps[q] = kept
            found[q] = swap(out, "cell", bits[at + 1])
        else:
            keeps[q] = stats(keeps[q], line(found[q]), parts["sums"].end(), spatial, mask8, onehot, q)
            line.mark(keeps[q][0])

    def own_exps():
        *parts["m"], sums = exp_split(line(logits), True)
        line.mark(sums)
        parts["sums"] = Total(line, sums, "cell", [*range(1, cell_bits), 0])

    def other_exps():
        parts["p"] = exp_split(line(other_logits), False)
        line.mark(parts["p"][0])

    def masses():
        parts["mass"] = mass_rows(line(parts["sums"].end()), parts["m"])
        line.mark(parts["mass"])

    if generic:
        own_exps()
        for q in range(number):
            make("both", q)
        masses(), other_exps()
        for _ in range(cell_bits):
            for q in range(number):
                step(q)
    else:
        make("send", 0), own_exps(), make("send", 2), parts["sums"].next(), make("keep", 0)
        parts["sums"].next(), step(0), make("across", 1), make("both", 3), make("keep", 2), step(2)
        step(0), step(1), other_exps(), step(2), step(3), step(0), masses()
        step(1), step(2), step(3), step(1), step(3)
    sums, mparts, pparts = parts["sums"].end(), parts["m"], parts["p"]
    preds = [keeps[q][0] for q in range(number)]
    spot_stats = [keeps[q][1] for q in range(number)]
    gene_stats = sum(keeps[q][2] for q in range(number))
    spot_stats = add_all(jnp.concatenate(spot_stats, axis=1), "cell")
    mass = parts["mass"][:1].reshape(-1, shard)
    joint = add_all(jnp.concatenate([gene_stats, mass], axis=0), "spot")
    gene_stats = joint[:24]
    mass = joint[24:].reshape(1, rows) / spots_total
    density_part = -jnp.sum(jnp.log(cells_total * mass)) / cells_total
    dens = jnp.broadcast_to(-1.0 / (cells_total * spots_total * mass), (8, rows))

    heights = (shard // 4,) * 4
    *grads, inner, losses = gradient(
        preds, sums, spatial, mask8, onehot, counts8, gene_stats, spot_stats, heights, slides, spots_total
    )

    blocks = spots_n // 2
    far_w = jnp.arange(blocks, dtype=jnp.int32)[:, None] << 1
    wanted = ((mine ^ far_w) * per_block + jnp.arange(per_block, dtype=jnp.int32)[None, :]) ^ me
    wanted = wanted.reshape(-1)
    place = reverse(wanted, cell_bits)
    low_bits = cell_bits - block_bits - 1
    short = ((place >> (low_bits + 1)) << low_bits) | (place & ((1 << low_bits) - 1))
    ids = jnp.concatenate([place, short]).astype(jnp.int32)
    core_bit = ((me >> block_bits) ^ mine) & 1

    line.mark(grads[0])
    number = len(heights)
    nears, fars, gots, acrosses, pairs, arrived = {}, {}, {}, {}, {}, {}

    def widen(q, bits):
        for bit in bits:
            if q in gots:
                nears[q] = glue(nears[q], line(gots[q]))
                line.mark(nears[q])
            else:
                nears[q] = line(nears[q])
            gots[q] = swap(nears[q], "cell", bit)

    def share(q):
        fars[q] = line(gots[q])
        size = heights[q] << low_bits
        out = pick(1 - core_bit.reshape(1), 1 << (block_bits - 1), size, nears[q], fars[q])
        line.mark(out)
        acrosses[q] = swap(out, "spot", 0)

    def multiply(q):
        outs = expr_part(
            ids, nears[q], fars[q], line(acrosses[q]), mparts, pparts, heights[q], blocks, wanted.size
        )
        outs = list(outs)
        line.mark(outs[0])
        bit = spots_n.bit_length() - 2
        while len(outs) > 2:
            half = len(outs) // 2
            came = swap(jnp.concatenate(outs[half:], axis=1), "spot", bit)
            came = jnp.split(came, half, axis=1)
            outs = [a + b for a, b in zip(outs[:half], came)]
            bit -= 1
        arrived[q] = swap(outs[1], "spot", bit)
        pairs[q] = (outs[0], arrived[q])

    nears.update(enumerate(grads))
    def first(q):
        widen(q, [cell_bits - 1])

    def second(q):
        widen(q, range(cell_bits - 2, 0, -1))

    def third(q):
        widen(q, [0])

    def pull():
        added = inner + pull_cols(line(dens), sums, mparts)
        added = jnp.concatenate(
            [added, jnp.broadcast_to(density_part - losses[0, 0], (8, 128))], axis=1
        )
        line.mark(added)
        parts["tail"] = Total(line, added, "cell", range(cell_bits - 1, -1, -1))

    spot_bits = range(spots_n.bit_length() - 1)
    parts["spots"] = Total(line, jnp.broadcast_to(losses[0, 1], (8, 128)), "spot", spot_bits)
    first(0), parts["spots"].next(), pull(), parts["spots"].next(), second(0), first(1), third(0)
    parts["tail"].next(), second(1), first(2), parts["tail"].next(), third(1), second(2), first(3)
    share(0), multiply(0), third(2), second(3), share(1), multiply(1), third(3), parts["tail"].next()
    line.also(arrived[0])
    share(2), multiply(2)
    line.also(arrived[1])
    share(3), multiply(3)
    tail = parts["tail"].end()
    loss = tail[0, cols] - parts["spots"].end()[0, 0]
    pairs = [pairs[q] for q in range(number)]
    gathered = [v for q in range(number) for v in (nears[q], fars[q])]

    logit_grad = logit_part(
        order, line(dens), sums, tail[:, :cols], source, mparts, gathered, heights, cells, unit, scale
    )
    expr_grad = join(pairs, heights, per_block, scale)
    return (loss, logit_grad, expr_grad)


def solution(mesh):
    placed = (P("cell", "spot"), P("cell", None), P("cell", "spot"), P(), P("spot"), P())
    return jax.shard_map(
        on_device,
        mesh=mesh,
        in_specs=placed,
        out_specs=(P(), P("cell", "spot"), P("cell", "spot")),
        check_vma=False,
    )
```

```python
import functools

import jax
import jax.numpy as jnp
from jax import lax
from jax.experimental import pallas as pl
from jax.experimental.pallas import tpu as pltpu
from jax.sharding import PartitionSpec as P

eps = 1e-06
F32 = jnp.float32
BF16 = jnp.bfloat16
MIB = 1024 * 1024


def shape_of(*dims, dtype=F32):
    return jax.ShapeDtypeStruct(dims, dtype)


def hbm(*dims):
    return pltpu.HBM(dims[:-1], dims[-1])


def after(value, *others):
    return lax.optimization_barrier((value, *others))[0]


def params(mib):
    return pltpu.CompilerParams(vmem_limit_bytes=mib * MIB)


def split(v):
    high = v.astype(BF16)
    return high, (v - high.astype(F32)).astype(BF16)


def dot(a, b, ca, cb, precision=None):
    return lax.dot_general(
        a, b, (((ca,), (cb,)), ((), ())), precision=precision, preferred_element_type=F32
    )


def dot3(ah, al, bh, bl, ca, cb):
    return dot(ah, bh, ca, cb) + dot(al, bh, ca, cb) + dot(ah, bl, ca, cb)


def exact(a, b, ca, cb):
    return dot(a, b, ca, cb, lax.Precision.HIGHEST)


def cost(flops, nbytes):
    return pl.CostEstimate(flops=0, bytes_accessed=0, transcendentals=0)


def simple(body, outs, *args, prefetch=None):
    def spec(v):
        return pl.BlockSpec(v.shape, lambda i, *_: (0,) * len(v.shape))

    number = 0 if prefetch is None else 1
    return pl.pallas_call(
        body,
        grid_spec=pltpu.PrefetchScalarGridSpec(
            num_scalar_prefetch=number,
            grid=(1,),
            in_specs=[spec(a) for a in args],
            out_specs=[spec(o) for o in outs],
        ),
        out_shape=list(outs),
        compiler_params=params(32),
        cost_estimate=cost(0, 0),
    )(*([] if prefetch is None else [prefetch]), *args)


def add_body(a, b, out):
    out[...] = a[...] + b[...]


def add(a, b):
    return simple(add_body, [shape_of(*a.shape)], a, b)[0]


def add_split_body(kept, came, low, high):
    if len(kept.shape) == 3:
        low[...], high[...] = kept[0] + came[0], kept[1] + came[1]
    else:
        half = kept.shape[1] // 2
        low[...] = kept[:, :half] + came[:, :half]
        high[...] = kept[:, half:] + came[:, half:]


def add_split(kept, came):
    rows, cols = kept.shape[-2:]
    out = shape_of(rows, cols if kept.ndim == 3 else cols // 2)
    return simple(add_split_body, [out, out], kept, came)


def glue_body(*refs):
    *sources, out = refs
    at = 0
    for source in sources:
        out[at : at + source.shape[0], :] = source[...]
        at += source.shape[0]


def glue(*parts):
    return simple(glue_body, [shape_of(sum(p.shape[0] for p in parts), parts[0].shape[1])], *parts)[0]


def pick_body(outer, size, which, *refs):
    *sources, out = refs
    at = 0
    for source in sources:
        for n in range(outer):
            start = pl.multiple_of((2 * n + which[0]) * size, 8)
            out[at : at + size, :] = source[pl.ds(start, size), :]
            at += size


def pick(which, outer, size, *sources):
    out = shape_of(outer * size * len(sources), sources[0].shape[1])
    body = functools.partial(pick_body, outer, size)
    return simple(body, [out], *sources, prefetch=which)[0]


def exp_body(with_sums, logits, high, low, *sums):
    vals = jnp.exp(logits[...])
    high[...], low[...] = split(vals)
    if with_sums:

        @pl.when(pl.program_id(0) == 0)
        def _():
            sums[0][...] = jnp.zeros_like(sums[0])

        sums[0][...] += jnp.sum(vals.reshape(-1, 8, vals.shape[1]), axis=0)


def exp_split(logits, with_sums):
    rows, cols = logits.shape
    step = 1024
    tile = pl.BlockSpec((step, cols), lambda i: (i, 0))
    outs, shapes = [tile, tile], [hbm(rows, cols, BF16)] * 2
    if with_sums:
        outs += [pl.BlockSpec((8, cols), lambda i: (0, 0))]
        shapes += [shape_of(8, cols)]
    return pl.pallas_call(
        functools.partial(exp_body, with_sums),
        grid=(rows // step,),
        in_specs=[tile],
        out_specs=outs,
        out_shape=shapes,
        compiler_params=params(56),
        cost_estimate=cost(rows * cols * 10, rows * cols * 8),
    )(logits)


def mass_body(sums, mh, ml, out):
    inv = 1.0 / jnp.sum(sums[...], axis=0, keepdims=True)
    ih, il = split(jnp.broadcast_to(inv, (8, inv.shape[1])))
    out[...] = dot3(ih, il, mh[...], ml[...], 1, 1)


def mass_rows(sums, mparts):
    rows, cols = mparts[0].shape
    step = 512
    tile = pl.BlockSpec((step, cols), lambda i: (i, 0))
    return pl.pallas_call(
        mass_body,
        grid=(rows // step,),
        in_specs=[pl.BlockSpec((8, cols), lambda i: (0, 0)), tile, tile],
        out_specs=pl.BlockSpec((8, step), lambda i: (0, i)),
        out_shape=shape_of(8, rows),
        compiler_params=params(56),
        cost_estimate=cost(rows * cols * 48, rows * cols * 4),
    )(sums, *mparts)


def below(total, shard, count):
    if total.shape[1] < shard:
        total = jnp.concatenate([total, jnp.zeros((1, shard - total.shape[1]), F32)], axis=1)
    lines = [total[:, at : at + shard] for at in range(0, total.shape[1], shard)]
    rows = jnp.concatenate(lines + [jnp.zeros((8 - len(lines), shard), F32)], axis=0)
    return jnp.concatenate([rows] * count, axis=1)


def predict_body(shard, given, widths, send_only, order, *refs):
    refs = list(refs)
    if given:
        gh, gl, gtotal = refs[:3]
        refs = refs[3:]
    if widths:
        logits, refs = refs[0], refs[1:]
    near = None if send_only else refs.pop(0)
    far = refs.pop(0) if widths else None
    if widths:
        total, refs = refs[-1], refs[:-1]
        th, tl, refs = refs[-2], refs[-1], refs[:-2]

        @pl.when(pl.program_id(0) == 0)
        def _():
            vals = jnp.exp(logits[...])
            total[...] = jnp.broadcast_to(jnp.sum(vals, axis=0, keepdims=True), total.shape)
            th[...], tl[...] = split(jnp.transpose(vals))

    count = (far if near is None else near).shape[1] // shard
    outs = iter(refs)
    if not send_only:
        near = split(near[...])
    if widths:
        far = split(far[...])
    if given:
        out, width = next(outs), gh.shape[0]
        out[:width] = dot3(gh[...], gl[...], *near, 1, 0)
        out[width:] = below(gtotal[:1], shard, count)
    if widths:
        kept = None if send_only else dot3(th[...], tl[...], *near, 1, 0)
        sent = dot3(th[...], tl[...], *far, 1, 0)
        at = 0
        for width in widths:
            rows = below(total[:1, at : at + width], shard, count)
            for vals in (kept, sent):
                if vals is not None:
                    out = next(outs)
                    out[:width] = vals[at : at + width]
                    out[width:] = rows
            at += width


def predict(order, expression, unit, shard, given, logits, start, widths, send_only=False):
    rows, genes = expression.shape
    count = genes // 2 // unit
    args, ins = [], []
    outs, shapes, scratch = [], [], []

    def add_out(width):
        outs.append(pl.BlockSpec((width + 8, unit), lambda i, order: (0, i)))
        shapes.append(shape_of(width + 8, genes // 2))

    if given is not None:
        width = given[0].shape[0]
        args += given
        ins += [pl.BlockSpec((width, rows), lambda i, order: (0, 0))] * 2
        ins += [pl.BlockSpec((8, width), lambda i, order: (0, 0))]
        add_out(width)
    wide = sum(widths)
    if widths:
        args.append(logits)
        ins.append(pl.BlockSpec((rows, wide), lambda i, order: (0, start // wide)))
        for width in widths:
            for _ in range(1 if send_only else 2):
                add_out(width)
    if not send_only:
        args.append(expression)
        ins.append(pl.BlockSpec((rows, unit), lambda i, order: (0, order[i])))
    if widths:
        args.append(expression)
        ins.append(pl.BlockSpec((rows, unit), lambda i, order: (0, order[count + i])))
        if send_only:
            outs += [pl.BlockSpec((wide, rows), lambda i, order: (0, 0))] * 2
            outs += [pl.BlockSpec((8, wide), lambda i, order: (0, 0))]
            shapes += [hbm(wide, rows, BF16)] * 2 + [shape_of(8, wide)]
        else:
            scratch = [pltpu.VMEM((wide, rows), BF16)] * 2 + [pltpu.VMEM((8, wide), F32)]
    return pl.pallas_call(
        functools.partial(predict_body, shard, given is not None, widths, send_only),
        grid_spec=pltpu.PrefetchScalarGridSpec(
            num_scalar_prefetch=1, grid=(count,), in_specs=ins, out_specs=outs, scratch_shapes=scratch
        ),
        out_shape=shapes,
        compiler_params=params(60),
        cost_estimate=cost(0, 0),
    )(order, *args)


def stats_body(width, kept, came, spatial, mask, onehot, pred, spots, genes, totals):
    vals = kept[...] + came[...]
    lines = max(1, width // vals.shape[1])
    total = jnp.concatenate([vals[width + n : width + n + 1] for n in range(lines)], axis=1)
    total = total[:, :width]
    totals[...] = jnp.concatenate([total, jnp.zeros((7, width), F32)], axis=0)
    vals = jnp.transpose(vals[:width]) / total
    pred[...] = vals
    spat = spatial[...]
    seen = dot(mask[...].astype(BF16), onehot[...].astype(BF16), 0, 0)
    terms = (vals * spat, vals * vals, spat * spat)
    rows = [jnp.sum(seen * t, axis=0, keepdims=True) for t in terms]
    spots[...] = jnp.concatenate(rows + [jnp.zeros((5, rows[0].shape[1]), F32)], axis=0)
    genes[...] = jnp.concatenate([exact(onehot[...], t, 1, 1) for t in terms], axis=0)


def stats(kept, came, spatial, mask, onehot, column, width):
    shard = kept.shape[1]
    strip = pl.BlockSpec((8, width), lambda i: (0, column))
    once = pl.BlockSpec((8, width), lambda i: (0, 0))
    given = pl.BlockSpec(kept.shape, lambda i: (0, 0))
    return pl.pallas_call(
        functools.partial(stats_body, width),
        grid=(1,),
        in_specs=[
            given,
            given,
            pl.BlockSpec((shard, width), lambda i: (0, column)),
            pl.BlockSpec((8, shard), lambda i: (0, 0)),
            strip,
        ],
        out_specs=[
            pl.BlockSpec((shard, width), lambda i: (0, 0)),
            once,
            pl.BlockSpec((24, shard), lambda i: (0, 0)),
            once,
        ],
        out_shape=[shape_of(shard, width), shape_of(8, width), shape_of(24, shard), shape_of(8, width)],
        compiler_params=params(32),
        cost_estimate=cost(0, 0),
    )(kept, came, spatial, mask, onehot)


def grad_body(slides, spots_total, parts, *refs):
    preds = refs[:parts]
    sums, spatial, mask, onehot, counts, gene_sums, spot_sums = refs[parts : parts + 7]
    outs = refs[parts + 7 : -2]
    inner, losses = refs[-2:]
    size = mask.shape[1]
    dot_g, pp_g, gg_g = (gene_sums[8 * i : 8 * i + 8, :] for i in range(3))
    norm_p, norm_s = jnp.sqrt(pp_g + eps), jnp.sqrt(gg_g + eps)
    weights = mask[...] / counts[...][:, :1]
    gene_part = jnp.sum(weights * (dot_g / (norm_p * norm_s))) / slides
    gene_weight = -weights / slides
    coef_s = gene_weight / (norm_p * norm_s)
    coef_p = gene_weight * dot_g / (norm_p * norm_p * norm_p * norm_s)
    a, b, c = (spot_sums[i : i + 1, :] for i in range(3))
    near_p, near_s = jnp.sqrt(b + eps), jnp.sqrt(c + eps)
    spot_part = jnp.sum(a / (near_p * near_s)) / spots_total
    edge_s = (-1.0 / spots_total) / (near_p * near_s)
    edge_p = (-1.0 / spots_total) * a / (near_p * near_p * near_p * near_s)
    total = jnp.sum(sums[...], axis=0, keepdims=True)
    hot = onehot[...]
    seen = dot(mask[...].astype(BF16), hot.astype(BF16), 0, 0)
    pred = jnp.concatenate([r[...] for r in preds], axis=1)
    grad = spatial[...] * (exact(coef_s, hot, 0, 0) + seen * edge_s) - pred * (
        exact(coef_p, hot, 0, 0) + seen * edge_p
    )
    row = jnp.sum(pred * grad, axis=0, keepdims=True)
    inner[...] = jnp.broadcast_to(row, inner.shape)
    grad = grad / total
    start = 0
    for out in outs:
        out[...] = grad[start : start + out.shape[0]]
        start += out.shape[0]
    lane = lax.broadcasted_iota(jnp.int32, losses.shape, 1)
    losses[...] = jnp.where(lane == 0, gene_part, jnp.where(lane == 1, spot_part, 0.0))


def gradient(preds, sums, spatial, mask, onehot, counts, gene_sums, spot_sums, heights, slides, spots_total):
    shard, cols = spatial.shape
    args = (*preds, sums, spatial, mask, onehot, counts, gene_sums, spot_sums)
    outs = [shape_of(h, cols) for h in heights] + [shape_of(8, cols), shape_of(8, 128)]
    return pl.pallas_call(
        functools.partial(grad_body, float(slides), float(spots_total), len(preds)),
        grid=(1,),
        in_specs=[pl.BlockSpec(a.shape, lambda i: (0, 0)) for a in args],
        out_specs=[pl.BlockSpec(o.shape, lambda i: (0, 0)) for o in outs],
        out_shape=outs,
        compiler_params=params(40),
        cost_estimate=cost(shard * cols * 60, shard * cols * 12),
    )(*args)


def pull_body(dens, sums, mh, ml, out):
    dh, dl = split(jnp.broadcast_to(dens[...][:1], dens.shape))

    @pl.when(pl.program_id(0) == 0)
    def _():
        out[...] = jnp.zeros_like(out)

    out[...] += dot3(dh, dl, mh[...], ml[...], 1, 0) / jnp.sum(sums[...], axis=0, keepdims=True)


def pull_cols(dens, sums, mparts):
    rows, cols = mparts[0].shape
    step = 512
    tile = pl.BlockSpec((step, cols), lambda i: (i, 0))
    strip = pl.BlockSpec((8, cols), lambda i: (0, 0))
    return pl.pallas_call(
        pull_body,
        grid=(rows // step,),
        in_specs=[pl.BlockSpec((8, step), lambda i: (0, i)), strip, tile, tile],
        out_specs=strip,
        out_shape=shape_of(8, cols),
        compiler_params=params(56),
        cost_estimate=cost(rows * cols * 48, rows * cols * 4),
    )(dens, sums, *mparts)


def expr_body(number, height, half, ids, near, far, across, mh, ml, ph, pls, *refs):
    outs, (oh, ol, ch, cl) = refs[:-4], refs[-4:]

    @pl.when(pl.program_id(0) == 0)
    def _():
        for n in range(number):
            at = ids[n]
            inside = pl.ds(pl.multiple_of((at % half) * height, 16), height)
            own = jnp.where(at < half, near[inside, :], far[inside, :])
            other = across[pl.ds(pl.multiple_of(ids[number + n] * height, 16), height), :]
            put = slice(n * height, (n + 1) * height)
            oh[put, :], ol[put, :] = split(own)
            ch[put, :], cl[put, :] = split(other)

    vals = dot3(mh[...], ml[...], oh[...], ol[...], 1, 1) + dot3(
        ph[...], pls[...], ch[...], cl[...], 1, 1
    )
    width = vals.shape[1] // len(outs)
    for n, out in enumerate(outs):
        out[...] = vals[:, n * width : (n + 1) * width]


def expr_part(ids, near, far, across, mparts, pparts, height, blocks, number):
    rows, cols = mparts[0].shape
    step = 512
    half = near.shape[0] // height
    tile = pl.BlockSpec((step, cols), lambda i, ids: (i, 0))
    width = number * height // blocks
    return pl.pallas_call(
        functools.partial(expr_body, number, height, half),
        grid_spec=pltpu.PrefetchScalarGridSpec(
            num_scalar_prefetch=1,
            grid=(rows // step,),
            in_specs=[pl.BlockSpec(a.shape, lambda i, ids: (0, 0)) for a in (near, far, across)]
            + [tile] * 4,
            out_specs=[pl.BlockSpec((step, width), lambda i, ids: (i, 0))] * blocks,
            scratch_shapes=[pltpu.VMEM((number * height, cols), BF16)] * 4,
        ),
        out_shape=[shape_of(rows, width)] * blocks,
        compiler_params=params(48),
        cost_estimate=cost(12 * rows * cols * number * height, rows * cols * 8),
    )(ids, near, far, across, *mparts, *pparts)


def logit_body(pieces, heights, unit, offset, scale, final, added, order, *refs):
    if final:
        dens, sums, inner, *refs = refs
    source, mh, ml, *refs = refs
    if added:
        part, *refs = refs
    grads, (out, dh, dl) = refs[:-3], refs[-3:]
    high = sum(heights)

    @pl.when(pl.program_id(0) == 0)
    def _():
        for p in range(pieces):
            base = order[p] * high
            at = 0
            for q, height in enumerate(heights):
                grad = grads[2 * q + (p >= pieces // 2)]
                inside = p % (pieces // 2)
                rows = pl.ds(pl.multiple_of(base + at, 16), height)
                dh[rows, :], dl[rows, :] = split(grad[inside * height : (inside + 1) * height, :])
                at += height

    if offset is None:
        vals = source[...]
    else:
        vals = jnp.concatenate(
            [source[:, p * unit + offset : p * unit + offset + high] for p in range(pieces)], axis=1
        )
    vals = dot3(*split(vals), dh[...], dl[...], 1, 0)
    if added:
        vals = vals + part[...]
    if final:
        inv = 1.0 / jnp.sum(sums[...], axis=0, keepdims=True)
        column = jnp.transpose(dens[...])[:, :1]
        vals = vals + (column - inner[...][:1]) * inv
        vals = (mh[...].astype(F32) + ml[...].astype(F32)) * vals * scale
    out[...] = vals


def logit_part(order, ends, expression, mparts, part, grads, heights, offset, pieces, unit, scale):
    rows, cols = mparts[0].shape
    genes = expression.shape[1]
    step = 256
    strip = pl.BlockSpec((8, cols), lambda i, order: (0, 0))
    tile = pl.BlockSpec((step, cols), lambda i, order: (i, 0))
    added, final = part is not None, ends is not None
    ins = [pl.BlockSpec((step, genes), lambda i, order: (i, 0)), tile, tile]
    args = [expression, *mparts]
    if final:
        ins = [pl.BlockSpec((8, step), lambda i, order: (0, i)), strip, strip] + ins
        args = [*ends, *args]
    if added:
        ins.append(tile)
        args.append(part)
    for g in grads:
        ins.append(pl.BlockSpec(g.shape, lambda i, order: (0, 0), pipeline_mode=pl.Buffered(1)))
    return pl.pallas_call(
        functools.partial(logit_body, pieces, heights, unit, offset, scale, final, added),
        grid_spec=pltpu.PrefetchScalarGridSpec(
            num_scalar_prefetch=1,
            grid=(rows // step,),
            in_specs=ins,
            out_specs=tile,
            scratch_shapes=[pltpu.VMEM((pieces * sum(heights), cols), BF16)] * 2,
        ),
        out_shape=shape_of(rows, cols),
        compiler_params=params(56),
        cost_estimate=cost(0, 0),
    )(order, *args, *grads)


def join_body(shards, heights, scale, *refs):
    out = refs[-1]
    shard = sum(heights)
    at = 0
    for q, height in enumerate(heights):
        vals = (refs[2 * q][...] + refs[2 * q + 1][...]) * scale
        for b in range(shards):
            out[:, b * shard + at : b * shard + at + height] = vals[:, b * height : (b + 1) * height]
        at += height


def join(pairs, heights, shards, scale):
    flat = [v for pair in pairs for v in pair]
    rows = flat[0].shape[0]
    step = 512
    genes = shards * sum(heights)
    return pl.pallas_call(
        functools.partial(join_body, shards, heights, scale),
        grid=(rows // step,),
        in_specs=[pl.BlockSpec((step, v.shape[1]), lambda i: (i, 0)) for v in flat],
        out_specs=pl.BlockSpec((step, genes), lambda i: (i, 0)),
        out_shape=shape_of(rows, genes),
        compiler_params=params(32),
        cost_estimate=cost(rows * genes * 2, rows * genes * 12),
    )(*flat)


class Line:
    def __init__(self):
        self.held = []

    def __call__(self, value):
        return after(value, *self.held) if self.held else value

    def mark(self, value):
        self.held = [value]

    def also(self, value):
        self.held = self.held + [value]


class Total:
    def __init__(self, line, value, axis, bits):
        self.line, self.value, self.axis, self.bits = line, value, axis, list(bits)
        self.come = swap(value, axis, self.bits.pop(0))

    def next(self):
        self.value = add(self.value, self.line(self.come))
        self.line.mark(self.value)
        self.come = swap(self.value, self.axis, self.bits.pop(0)) if self.bits else None

    def end(self):
        while self.come is not None:
            self.next()
        return self.value


def swap(v, axis, bit):
    size = lax.axis_size(axis)
    return lax.ppermute(v, axis, [(i, i ^ (1 << bit)) for i in range(size)])


def add_all(v, axis):
    for bit in range(lax.axis_size(axis).bit_length() - 1):
        v = add(v, swap(v, axis, bit))
    return v


def reverse(value, bits):
    return sum(((value >> b) & 1) << (bits - 1 - b) for b in range(bits))


def on_device(logits, expression, spatial, masks, slide_ids, counts):
    cells, spots_n = lax.axis_size("cell"), lax.axis_size("spot")
    me, mine = lax.axis_index("cell"), lax.axis_index("spot")
    rows, cols = logits.shape
    shard = spatial.shape[0]
    slides, genes = masks.shape
    cells_total, spots_total = rows * cells, cols * spots_n
    cell_bits = cells.bit_length() - 1
    per_block = cells // spots_n
    block_bits = per_block.bit_length() - 1
    scale = float(cells_total * spots_total)

    other_logits = swap(logits, "spot", 0)
    order = me ^ reverse(jnp.arange(cells, dtype=jnp.int32), cell_bits)
    unit = 256
    source, blocks_order = expression, order
    if shard != unit:
        source = source.reshape(rows, cells, shard)[:, order].reshape(rows, genes)
        blocks_order = jnp.arange(genes // unit, dtype=jnp.int32)
        order = jnp.arange(cells, dtype=jnp.int32)

    mask8 = jnp.pad(masks.astype(F32), ((0, 8 - slides), (0, 0)))
    mask8 = lax.dynamic_slice_in_dim(mask8, me * shard, shard, 1)
    onehot = (slide_ids[None, :] == jnp.arange(8, dtype=jnp.int32)[:, None]).astype(F32)
    counts8 = jnp.broadcast_to(
        jnp.pad(counts.astype(F32), (0, 8 - slides), constant_values=1.0)[:, None], (8, 128)
    )

    line = Line()

    widths = (256, 256, 256, 128, 128)
    starts = [sum(widths[:q]) for q in range(len(widths))]
    generic = cell_bits != 3
    piece = min(shard, unit)
    keeps, steps, found, parts = {}, {}, {}, {}

    def make(*chunks, given=None):
        outs = predict(
            blocks_order,
            source,
            unit,
            piece,
            given,
            line(logits),
            starts[chunks[0]],
            tuple(widths[q] for q in chunks),
        )
        line.mark(outs[0])
        if given is not None:
            keeps[chunks[0] - 1], *outs = outs
        for n, q in enumerate(chunks):
            keeps[q] = outs[2 * n]
            found[q] = swap(outs[2 * n + 1], "cell", 0)

    def step(q):
        at = steps.get(q, 0)
        steps[q] = at + 1
        came = line(found[q])
        if at < cell_bits - 1:
            keeps[q], out = add_split(keeps[q], came)
            line.mark(out)
            found[q] = swap(out, "cell", at + 1)
        else:
            keeps[q] = stats(
                keeps[q], came, spatial, mask8, onehot, starts[q] // widths[q], widths[q]
            )
            line.mark(keeps[q][0])

    def own_exps():
        parts["m"] = exp_split(line(logits), False)
        line.mark(parts["m"][0])

    def other_exps():
        parts["p"] = exp_split(line(other_logits), False)
        line.mark(parts["p"][0])

    def masses():
        mass = mass_rows(line(sums), parts["m"])
        mass = jnp.concatenate([mass, jnp.broadcast_to(losses[0, 1], (8, 128))], axis=1)
        line.mark(mass)
        parts["mass"] = Total(line, mass, "spot", range(spots_n.bit_length() - 1))

    out, *first = predict(
        blocks_order, source, unit, piece, None, logits, 0, widths[:1], send_only=True
    )
    line.mark(out)
    found[0] = swap(out, "cell", 0)
    make(1, given=first)
    own_exps()
    if generic:
        make(2), make(3, 4), other_exps()
        for _ in range(cell_bits):
            for q in range(len(widths)):
                step(q)
    else:
        step(0), make(2), step(0), step(1), make(3, 4), step(0), step(1), step(2)
        other_exps(), step(2), step(3), step(1), step(4), step(3), step(2), step(4)
        step(3), step(4)
    number = len(widths)
    sums = jnp.concatenate([keeps[q][3] for q in range(number)], axis=1)
    mparts, pparts = parts["m"], parts["p"]
    preds = [keeps[q][0] for q in range(number)]
    spot_stats = [keeps[q][1] for q in range(number)]
    gene_stats = sum(keeps[q][2] for q in range(number))
    spot_stats = Total(line, jnp.concatenate(spot_stats, axis=1), "cell", range(cell_bits))
    gene_stats = Total(line, gene_stats, "spot", range(spots_n.bit_length() - 1))
    for _ in range(2):
        gene_stats.next(), spot_stats.next()
    gene_stats, spot_stats = gene_stats.end(), spot_stats.end()

    heights = (shard // 4,) * 4
    *grads, inner, losses = gradient(
        preds, sums, spatial, mask8, onehot, counts8, gene_stats, spot_stats, heights, slides, spots_total
    )

    blocks = spots_n // 2
    far_w = jnp.arange(blocks, dtype=jnp.int32)[:, None] << 1
    wanted = ((mine ^ far_w) * per_block + jnp.arange(per_block, dtype=jnp.int32)[None, :]) ^ me
    wanted = wanted.reshape(-1)
    place = reverse(wanted, cell_bits)
    low_bits = cell_bits - block_bits - 1
    short = ((place >> (low_bits + 1)) << low_bits) | (place & ((1 << low_bits) - 1))
    ids = jnp.concatenate([place, short]).astype(jnp.int32)
    core_bit = ((me >> block_bits) ^ mine) & 1

    line.mark(grads[0])
    number = len(heights)
    nears, fars, gots, acrosses, pairs, arrived = {}, {}, {}, {}, {}, {}

    def widen(q, bits):
        for bit in bits:
            if q in gots:
                nears[q] = glue(nears[q], line(gots[q]))
                line.mark(nears[q])
            else:
                nears[q] = line(nears[q])
            gots[q] = swap(nears[q], "cell", bit)

    def share(q):
        fars[q] = line(gots[q])
        size = heights[q] << low_bits
        out = pick(1 - core_bit.reshape(1), 1 << (block_bits - 1), size, nears[q], fars[q])
        line.mark(out)
        acrosses[q] = swap(out, "spot", 0)

    def multiply(q):
        outs = expr_part(
            ids, nears[q], fars[q], line(acrosses[q]), mparts, pparts, heights[q], blocks, wanted.size
        )
        outs = list(outs)
        line.mark(outs[0])
        bit = spots_n.bit_length() - 2
        while len(outs) > 2:
            half = len(outs) // 2
            came = swap(jnp.concatenate(outs[half:], axis=1), "spot", bit)
            came = jnp.split(came, half, axis=1)
            outs = [a + b for a, b in zip(outs[:half], came)]
            bit -= 1
        arrived[q] = swap(outs[1], "spot", bit)
        pairs[q] = (outs[0], arrived[q])

    nears.update(enumerate(grads))
    def first(q):
        widen(q, [cell_bits - 1])

    def second(q):
        widen(q, range(cell_bits - 2, 0, -1))

    def third(q):
        widen(q, [0])

    def pull():
        joint = parts["mass"].end()[:1]
        mass, parts["spots"] = joint[:, :rows] / spots_total, joint[0, rows]
        density_part = -jnp.sum(jnp.log(cells_total * mass)) / cells_total
        parts["dens"] = jnp.broadcast_to(-1.0 / (cells_total * spots_total * mass), (8, rows))
        added = inner + pull_cols(line(parts["dens"]), sums, mparts)
        added = jnp.concatenate(
            [added, jnp.broadcast_to(density_part - losses[0, 0], (8, 128))], axis=1
        )
        line.mark(added)
        parts["tail"] = Total(line, added, "cell", range(cell_bits - 1, -1, -1))

    def logits_of(chunks, ends, part, offset):
        grads_of = [v for q in chunks for v in (nears[q], fars[q])]
        size = [heights[q] for q in chunks]
        out = logit_part(
            order, ends, line(source), mparts, part, grads_of, size, offset, cells, unit, scale
        )
        line.mark(out)
        return out

    first(0), masses(), second(0), parts["mass"].next(), first(1), second(1), third(0), first(2)
    pull(), third(1), second(2), first(3), share(0), multiply(0), third(2), second(3)
    share(1), multiply(1), third(3), parts["tail"].next()
    line.also(arrived[0])
    share(2), multiply(2), parts["tail"].next()
    line.also(arrived[1])
    share(3), multiply(3)
    tail = parts["tail"].end()
    loss = tail[0, cols] - parts["spots"]
    pairs = [pairs[q] for q in range(number)]
    ends = parts["dens"], sums, tail[:, :cols]
    logit_grad = logits_of(range(number), ends, None, None)
    expr_grad = join(pairs, heights, per_block, scale)
    return (loss, logit_grad, expr_grad)


def solution(mesh):
    placed = (P("cell", "spot"), P("cell", None), P("cell", "spot"), P(), P("spot"), P())
    return jax.shard_map(
        on_device,
        mesh=mesh,
        in_specs=placed,
        out_specs=(P(), P("cell", "spot"), P("cell", "spot")),
        check_vma=False,
    )
```

```python
import functools

import jax
import jax.numpy as jnp
from jax import lax
from jax.experimental import pallas as pl
from jax.experimental.pallas import tpu as pltpu
from jax.sharding import PartitionSpec as P

eps = 1e-06
F32 = jnp.float32
BF16 = jnp.bfloat16
MIB = 1024 * 1024


def shape_of(*dims, dtype=F32):
    return jax.ShapeDtypeStruct(dims, dtype)


def hbm(*dims):
    return pltpu.HBM(dims[:-1], dims[-1])


def after(value, *others):
    return lax.optimization_barrier((value, *others))[0]


def params(mib):
    return pltpu.CompilerParams(vmem_limit_bytes=mib * MIB)


def split(v):
    high = v.astype(BF16)
    return high, (v - high.astype(F32)).astype(BF16)


def dot(a, b, ca, cb, precision=None):
    return lax.dot_general(
        a, b, (((ca,), (cb,)), ((), ())), precision=precision, preferred_element_type=F32
    )


def dot3(ah, al, bh, bl, ca, cb):
    return dot(ah, bh, ca, cb) + dot(al, bh, ca, cb) + dot(ah, bl, ca, cb)


def exact(a, b, ca, cb):
    return dot(a, b, ca, cb, lax.Precision.HIGHEST)


def cost(flops, nbytes):
    return pl.CostEstimate(flops=0, bytes_accessed=0, transcendentals=0)


def simple(body, outs, *args, prefetch=None):
    def spec(v):
        return pl.BlockSpec(v.shape, lambda i, *_: (0,) * len(v.shape))

    number = 0 if prefetch is None else 1
    return pl.pallas_call(
        body,
        grid_spec=pltpu.PrefetchScalarGridSpec(
            num_scalar_prefetch=number,
            grid=(1,),
            in_specs=[spec(a) for a in args],
            out_specs=[spec(o) for o in outs],
        ),
        out_shape=list(outs),
        compiler_params=params(32),
        cost_estimate=cost(0, 0),
    )(*([] if prefetch is None else [prefetch]), *args)


def add_body(a, b, out):
    out[...] = a[...] + b[...]


def add(a, b):
    return simple(add_body, [shape_of(*a.shape)], a, b)[0]


def add_split_body(kept, came, low, high):
    if len(kept.shape) == 3:
        low[...], high[...] = kept[0] + came[0], kept[1] + came[1]
    else:
        half = kept.shape[1] // 2
        low[...] = kept[:, :half] + came[:, :half]
        high[...] = kept[:, half:] + came[:, half:]


def add_split(kept, came):
    rows, cols = kept.shape[-2:]
    out = shape_of(rows, cols if kept.ndim == 3 else cols // 2)
    return simple(add_split_body, [out, out], kept, came)


def glue_body(*refs):
    *sources, out = refs
    at = 0
    for source in sources:
        out[at : at + source.shape[0], :] = source[...]
        at += source.shape[0]


def glue(*parts):
    return simple(glue_body, [shape_of(sum(p.shape[0] for p in parts), parts[0].shape[1])], *parts)[0]


def pick_body(outer, size, which, *refs):
    *sources, out = refs
    at = 0
    for source in sources:
        for n in range(outer):
            start = pl.multiple_of((2 * n + which[0]) * size, 8)
            out[at : at + size, :] = source[pl.ds(start, size), :]
            at += size


def pick(which, outer, size, *sources):
    out = shape_of(outer * size * len(sources), sources[0].shape[1])
    body = functools.partial(pick_body, outer, size)
    return simple(body, [out], *sources, prefetch=which)[0]


def exp_body(with_sums, logits, high, low, *sums):
    vals = jnp.exp(logits[...])
    high[...], low[...] = split(vals)
    if with_sums:

        @pl.when(pl.program_id(0) == 0)
        def _():
            sums[0][...] = jnp.zeros_like(sums[0])

        sums[0][...] += jnp.sum(vals.reshape(-1, 8, vals.shape[1]), axis=0)


def exp_split(logits, with_sums):
    rows, cols = logits.shape
    step = 1024
    tile = pl.BlockSpec((step, cols), lambda i: (i, 0))
    outs, shapes = [tile, tile], [hbm(rows, cols, BF16)] * 2
    if with_sums:
        outs += [pl.BlockSpec((8, cols), lambda i: (0, 0))]
        shapes += [shape_of(8, cols)]
    return pl.pallas_call(
        functools.partial(exp_body, with_sums),
        grid=(rows // step,),
        in_specs=[tile],
        out_specs=outs,
        out_shape=shapes,
        compiler_params=params(56),
        cost_estimate=cost(rows * cols * 10, rows * cols * 8),
    )(logits)


def mass_body(sums, mh, ml, out):
    inv = 1.0 / jnp.sum(sums[...], axis=0, keepdims=True)
    ih, il = split(jnp.broadcast_to(inv, (8, inv.shape[1])))
    out[...] = dot3(ih, il, mh[...], ml[...], 1, 1)


def mass_rows(sums, mparts):
    rows, cols = mparts[0].shape
    step = 512
    tile = pl.BlockSpec((step, cols), lambda i: (i, 0))
    return pl.pallas_call(
        mass_body,
        grid=(rows // step,),
        in_specs=[pl.BlockSpec((8, cols), lambda i: (0, 0)), tile, tile],
        out_specs=pl.BlockSpec((8, step), lambda i: (0, i)),
        out_shape=shape_of(8, rows),
        compiler_params=params(56),
        cost_estimate=cost(rows * cols * 48, rows * cols * 4),
    )(sums, *mparts)


def below(total, shard, count):
    if total.shape[1] < shard:
        total = jnp.concatenate([total, jnp.zeros((1, shard - total.shape[1]), F32)], axis=1)
    lines = [total[:, at : at + shard] for at in range(0, total.shape[1], shard)]
    rows = jnp.concatenate(lines + [jnp.zeros((8 - len(lines), shard), F32)], axis=0)
    return jnp.concatenate([rows] * count, axis=1)


def predict_body(shard, given, widths, send_only, order, *refs):
    refs = list(refs)
    if given:
        gh, gl, gtotal = refs[:3]
        refs = refs[3:]
    if widths:
        logits, refs = refs[0], refs[1:]
    near = None if send_only else refs.pop(0)
    far = refs.pop(0) if widths else None
    if widths:
        total, refs = refs[-1], refs[:-1]
        th, tl, refs = refs[-2], refs[-1], refs[:-2]

        @pl.when(pl.program_id(0) == 0)
        def _():
            vals = jnp.exp(logits[...])
            total[...] = jnp.broadcast_to(jnp.sum(vals, axis=0, keepdims=True), total.shape)
            th[...], tl[...] = split(jnp.transpose(vals))

    count = (far if near is None else near).shape[1] // shard
    outs = iter(refs)
    if not send_only:
        near = split(near[...])
    if widths:
        far = split(far[...])
    if given:
        out, width = next(outs), gh.shape[0]
        out[:width] = dot3(gh[...], gl[...], *near, 1, 0)
        out[width:] = below(gtotal[:1], shard, count)
    if widths:
        kept = None if send_only else dot3(th[...], tl[...], *near, 1, 0)
        sent = dot3(th[...], tl[...], *far, 1, 0)
        at = 0
        for width in widths:
            rows = below(total[:1, at : at + width], shard, count)
            for vals in (kept, sent):
                if vals is not None:
                    out = next(outs)
                    out[:width] = vals[at : at + width]
                    out[width:] = rows
            at += width


def predict(order, expression, unit, shard, given, logits, start, widths, send_only=False):
    rows, genes = expression.shape
    count = genes // 2 // unit
    args, ins = [], []
    outs, shapes, scratch = [], [], []

    def add_out(width):
        outs.append(pl.BlockSpec((width + 8, unit), lambda i, order: (0, i)))
        shapes.append(shape_of(width + 8, genes // 2))

    if given is not None:
        width = given[0].shape[0]
        args += given
        ins += [pl.BlockSpec((width, rows), lambda i, order: (0, 0))] * 2
        ins += [pl.BlockSpec((8, width), lambda i, order: (0, 0))]
        add_out(width)
    wide = sum(widths)
    if widths:
        args.append(logits)
        ins.append(pl.BlockSpec((rows, wide), lambda i, order: (0, start // wide)))
        for width in widths:
            for _ in range(1 if send_only else 2):
                add_out(width)
    if not send_only:
        args.append(expression)
        ins.append(pl.BlockSpec((rows, unit), lambda i, order: (0, order[i])))
    if widths:
        args.append(expression)
        ins.append(pl.BlockSpec((rows, unit), lambda i, order: (0, order[count + i])))
        if send_only:
            outs += [pl.BlockSpec((wide, rows), lambda i, order: (0, 0))] * 2
            outs += [pl.BlockSpec((8, wide), lambda i, order: (0, 0))]
            shapes += [hbm(wide, rows, BF16)] * 2 + [shape_of(8, wide)]
        else:
            scratch = [pltpu.VMEM((wide, rows), BF16)] * 2 + [pltpu.VMEM((8, wide), F32)]
    return pl.pallas_call(
        functools.partial(predict_body, shard, given is not None, widths, send_only),
        grid_spec=pltpu.PrefetchScalarGridSpec(
            num_scalar_prefetch=1, grid=(count,), in_specs=ins, out_specs=outs, scratch_shapes=scratch
        ),
        out_shape=shapes,
        compiler_params=params(60),
        cost_estimate=cost(0, 0),
    )(order, *args)


def stats_body(width, kept, came, spatial, mask, onehot, pred, spots, genes, totals):
    vals = kept[...] + came[...]
    lines = max(1, width // vals.shape[1])
    total = jnp.concatenate([vals[width + n : width + n + 1] for n in range(lines)], axis=1)
    total = total[:, :width]
    totals[...] = jnp.concatenate([total, jnp.zeros((7, width), F32)], axis=0)
    vals = jnp.transpose(vals[:width]) / total
    pred[...] = vals
    spat = spatial[...]
    seen = dot(mask[...].astype(BF16), onehot[...].astype(BF16), 0, 0)
    terms = (vals * spat, vals * vals, spat * spat)
    rows = [jnp.sum(seen * t, axis=0, keepdims=True) for t in terms]
    spots[...] = jnp.concatenate(rows + [jnp.zeros((5, rows[0].shape[1]), F32)], axis=0)
    genes[...] = jnp.concatenate([exact(onehot[...], t, 1, 1) for t in terms], axis=0)


def stats(kept, came, spatial, mask, onehot, column, width):
    shard = kept.shape[1]
    strip = pl.BlockSpec((8, width), lambda i: (0, column))
    once = pl.BlockSpec((8, width), lambda i: (0, 0))
    given = pl.BlockSpec(kept.shape, lambda i: (0, 0))
    return pl.pallas_call(
        functools.partial(stats_body, width),
        grid=(1,),
        in_specs=[
            given,
            given,
            pl.BlockSpec((shard, width), lambda i: (0, column)),
            pl.BlockSpec((8, shard), lambda i: (0, 0)),
            strip,
        ],
        out_specs=[
            pl.BlockSpec((shard, width), lambda i: (0, 0)),
            once,
            pl.BlockSpec((24, shard), lambda i: (0, 0)),
            once,
        ],
        out_shape=[shape_of(shard, width), shape_of(8, width), shape_of(24, shard), shape_of(8, width)],
        compiler_params=params(32),
        cost_estimate=cost(0, 0),
    )(kept, came, spatial, mask, onehot)


def grad_body(slides, spots_total, parts, *refs):
    preds = refs[:parts]
    sums, spatial, mask, onehot, counts, gene_sums, spot_sums = refs[parts : parts + 7]
    outs = refs[parts + 7 : -2]
    inner, losses = refs[-2:]
    size = mask.shape[1]
    dot_g, pp_g, gg_g = (gene_sums[8 * i : 8 * i + 8, :] for i in range(3))
    norm_p, norm_s = jnp.sqrt(pp_g + eps), jnp.sqrt(gg_g + eps)
    weights = mask[...] / counts[...][:, :1]
    gene_part = jnp.sum(weights * (dot_g / (norm_p * norm_s))) / slides
    gene_weight = -weights / slides
    coef_s = gene_weight / (norm_p * norm_s)
    coef_p = gene_weight * dot_g / (norm_p * norm_p * norm_p * norm_s)
    a, b, c = (spot_sums[i : i + 1, :] for i in range(3))
    near_p, near_s = jnp.sqrt(b + eps), jnp.sqrt(c + eps)
    spot_part = jnp.sum(a / (near_p * near_s)) / spots_total
    edge_s = (-1.0 / spots_total) / (near_p * near_s)
    edge_p = (-1.0 / spots_total) * a / (near_p * near_p * near_p * near_s)
    total = jnp.sum(sums[...], axis=0, keepdims=True)
    hot = onehot[...]
    seen = dot(mask[...].astype(BF16), hot.astype(BF16), 0, 0)
    pred = jnp.concatenate([r[...] for r in preds], axis=1)
    grad = spatial[...] * (exact(coef_s, hot, 0, 0) + seen * edge_s) - pred * (
        exact(coef_p, hot, 0, 0) + seen * edge_p
    )
    row = jnp.sum(pred * grad, axis=0, keepdims=True)
    inner[...] = jnp.broadcast_to(row, inner.shape)
    grad = grad / total
    start = 0
    for out in outs:
        out[...] = grad[start : start + out.shape[0]]
        start += out.shape[0]
    lane = lax.broadcasted_iota(jnp.int32, losses.shape, 1)
    losses[...] = jnp.where(lane == 0, gene_part, jnp.where(lane == 1, spot_part, 0.0))


def gradient(preds, sums, spatial, mask, onehot, counts, gene_sums, spot_sums, heights, slides, spots_total):
    shard, cols = spatial.shape
    args = (*preds, sums, spatial, mask, onehot, counts, gene_sums, spot_sums)
    outs = [shape_of(h, cols) for h in heights] + [shape_of(8, cols), shape_of(8, 128)]
    return pl.pallas_call(
        functools.partial(grad_body, float(slides), float(spots_total), len(preds)),
        grid=(1,),
        in_specs=[pl.BlockSpec(a.shape, lambda i: (0, 0)) for a in args],
        out_specs=[pl.BlockSpec(o.shape, lambda i: (0, 0)) for o in outs],
        out_shape=outs,
        compiler_params=params(40),
        cost_estimate=cost(shard * cols * 60, shard * cols * 12),
    )(*args)


def pull_body(dens, sums, mh, ml, out):
    dh, dl = split(jnp.broadcast_to(dens[...][:1], dens.shape))

    @pl.when(pl.program_id(0) == 0)
    def _():
        out[...] = jnp.zeros_like(out)

    out[...] += dot3(dh, dl, mh[...], ml[...], 1, 0) / jnp.sum(sums[...], axis=0, keepdims=True)


def pull_cols(dens, sums, mparts):
    rows, cols = mparts[0].shape
    step = 512
    tile = pl.BlockSpec((step, cols), lambda i: (i, 0))
    strip = pl.BlockSpec((8, cols), lambda i: (0, 0))
    return pl.pallas_call(
        pull_body,
        grid=(rows // step,),
        in_specs=[pl.BlockSpec((8, step), lambda i: (0, i)), strip, tile, tile],
        out_specs=strip,
        out_shape=shape_of(8, cols),
        compiler_params=params(56),
        cost_estimate=cost(rows * cols * 48, rows * cols * 4),
    )(dens, sums, *mparts)


def expr_body(number, height, half, ids, near, far, across, mh, ml, ph, pls, *refs):
    outs, (oh, ol, ch, cl) = refs[:-4], refs[-4:]

    @pl.when(pl.program_id(0) == 0)
    def _():
        for n in range(number):
            at = ids[n]
            inside = pl.ds(pl.multiple_of((at % half) * height, 16), height)
            own = jnp.where(at < half, near[inside, :], far[inside, :])
            other = across[pl.ds(pl.multiple_of(ids[number + n] * height, 16), height), :]
            put = slice(n * height, (n + 1) * height)
            oh[put, :], ol[put, :] = split(own)
            ch[put, :], cl[put, :] = split(other)

    vals = dot3(mh[...], ml[...], oh[...], ol[...], 1, 1) + dot3(
        ph[...], pls[...], ch[...], cl[...], 1, 1
    )
    width = vals.shape[1] // len(outs)
    for n, out in enumerate(outs):
        out[...] = vals[:, n * width : (n + 1) * width]


def expr_part(ids, near, far, across, mparts, pparts, height, blocks, number):
    rows, cols = mparts[0].shape
    step = 512
    half = near.shape[0] // height
    tile = pl.BlockSpec((step, cols), lambda i, ids: (i, 0))
    width = number * height // blocks
    return pl.pallas_call(
        functools.partial(expr_body, number, height, half),
        grid_spec=pltpu.PrefetchScalarGridSpec(
            num_scalar_prefetch=1,
            grid=(rows // step,),
            in_specs=[pl.BlockSpec(a.shape, lambda i, ids: (0, 0)) for a in (near, far, across)]
            + [tile] * 4,
            out_specs=[pl.BlockSpec((step, width), lambda i, ids: (i, 0))] * blocks,
            scratch_shapes=[pltpu.VMEM((number * height, cols), BF16)] * 4,
        ),
        out_shape=[shape_of(rows, width)] * blocks,
        compiler_params=params(48),
        cost_estimate=cost(12 * rows * cols * number * height, rows * cols * 8),
    )(ids, near, far, across, *mparts, *pparts)


def logit_body(pieces, heights, unit, offset, scale, final, added, order, *refs):
    if final:
        dens, sums, inner, *refs = refs
    source, mh, ml, *refs = refs
    if added:
        part, *refs = refs
    grads, (out, dh, dl) = refs[:-3], refs[-3:]
    high = sum(heights)

    @pl.when(pl.program_id(0) == 0)
    def _():
        for p in range(pieces):
            base = order[p] * high
            at = 0
            for q, height in enumerate(heights):
                grad = grads[2 * q + (p >= pieces // 2)]
                inside = p % (pieces // 2)
                rows = pl.ds(pl.multiple_of(base + at, 16), height)
                dh[rows, :], dl[rows, :] = split(grad[inside * height : (inside + 1) * height, :])
                at += height

    if offset is None:
        vals = source[...]
    else:
        vals = jnp.concatenate(
            [source[:, p * unit + offset : p * unit + offset + high] for p in range(pieces)], axis=1
        )
    vals = dot3(*split(vals), dh[...], dl[...], 1, 0)
    if added:
        vals = vals + part[...]
    if final:
        inv = 1.0 / jnp.sum(sums[...], axis=0, keepdims=True)
        column = jnp.transpose(dens[...])[:, :1]
        vals = vals + (column - inner[...][:1]) * inv
        vals = (mh[...].astype(F32) + ml[...].astype(F32)) * vals * scale
    out[...] = vals


def logit_part(order, ends, expression, mparts, part, grads, heights, offset, pieces, unit, scale):
    rows, cols = mparts[0].shape
    genes = expression.shape[1]
    step = 256
    strip = pl.BlockSpec((8, cols), lambda i, order: (0, 0))
    tile = pl.BlockSpec((step, cols), lambda i, order: (i, 0))
    added, final = part is not None, ends is not None
    ins = [pl.BlockSpec((step, genes), lambda i, order: (i, 0)), tile, tile]
    args = [expression, *mparts]
    if final:
        ins = [pl.BlockSpec((8, step), lambda i, order: (0, i)), strip, strip] + ins
        args = [*ends, *args]
    if added:
        ins.append(tile)
        args.append(part)
    for g in grads:
        ins.append(pl.BlockSpec(g.shape, lambda i, order: (0, 0), pipeline_mode=pl.Buffered(1)))
    return pl.pallas_call(
        functools.partial(logit_body, pieces, heights, unit, offset, scale, final, added),
        grid_spec=pltpu.PrefetchScalarGridSpec(
            num_scalar_prefetch=1,
            grid=(rows // step,),
            in_specs=ins,
            out_specs=tile,
            scratch_shapes=[pltpu.VMEM((pieces * sum(heights), cols), BF16)] * 2,
        ),
        out_shape=shape_of(rows, cols),
        compiler_params=params(56),
        cost_estimate=cost(0, 0),
    )(order, *args, *grads)


def join_body(shards, heights, scale, *refs):
    out = refs[-1]
    shard = sum(heights)
    at = 0
    for q, height in enumerate(heights):
        vals = (refs[2 * q][...] + refs[2 * q + 1][...]) * scale
        for b in range(shards):
            out[:, b * shard + at : b * shard + at + height] = vals[:, b * height : (b + 1) * height]
        at += height


def join(pairs, heights, shards, scale):
    flat = [v for pair in pairs for v in pair]
    rows = flat[0].shape[0]
    step = 512
    genes = shards * sum(heights)
    return pl.pallas_call(
        functools.partial(join_body, shards, heights, scale),
        grid=(rows // step,),
        in_specs=[pl.BlockSpec((step, v.shape[1]), lambda i: (i, 0)) for v in flat],
        out_specs=pl.BlockSpec((step, genes), lambda i: (i, 0)),
        out_shape=shape_of(rows, genes),
        compiler_params=params(32),
        cost_estimate=cost(rows * genes * 2, rows * genes * 12),
    )(*flat)


class Line:
    def __init__(self):
        self.held = []

    def __call__(self, value):
        return after(value, *self.held) if self.held else value

    def mark(self, value):
        self.held = [value]

    def also(self, value):
        self.held = self.held + [value]


class Total:
    def __init__(self, line, value, axis, bits):
        self.line, self.value, self.axis, self.bits = line, value, axis, list(bits)
        self.come = swap(value, axis, self.bits.pop(0))

    def next(self):
        self.value = add(self.value, self.line(self.come))
        self.line.mark(self.value)
        self.come = swap(self.value, self.axis, self.bits.pop(0)) if self.bits else None

    def end(self):
        while self.come is not None:
            self.next()
        return self.value


def swap(v, axis, bit):
    size = lax.axis_size(axis)
    return lax.ppermute(v, axis, [(i, i ^ (1 << bit)) for i in range(size)])


def add_all(v, axis):
    for bit in range(lax.axis_size(axis).bit_length() - 1):
        v = add(v, swap(v, axis, bit))
    return v


def reverse(value, bits):
    return sum(((value >> b) & 1) << (bits - 1 - b) for b in range(bits))


def on_device(logits, expression, spatial, masks, slide_ids, counts):
    cells, spots_n = lax.axis_size("cell"), lax.axis_size("spot")
    me, mine = lax.axis_index("cell"), lax.axis_index("spot")
    rows, cols = logits.shape
    shard = spatial.shape[0]
    slides, genes = masks.shape
    cells_total, spots_total = rows * cells, cols * spots_n
    cell_bits = cells.bit_length() - 1
    per_block = cells // spots_n
    block_bits = per_block.bit_length() - 1
    scale = float(cells_total * spots_total)

    other_logits = swap(logits, "spot", 0)
    order = me ^ reverse(jnp.arange(cells, dtype=jnp.int32), cell_bits)
    unit = 256
    source, blocks_order = expression, order
    if shard != unit:
        source = source.reshape(rows, cells, shard)[:, order].reshape(rows, genes)
        blocks_order = jnp.arange(genes // unit, dtype=jnp.int32)
        order = jnp.arange(cells, dtype=jnp.int32)

    mask8 = jnp.pad(masks.astype(F32), ((0, 8 - slides), (0, 0)))
    mask8 = lax.dynamic_slice_in_dim(mask8, me * shard, shard, 1)
    onehot = (slide_ids[None, :] == jnp.arange(8, dtype=jnp.int32)[:, None]).astype(F32)
    counts8 = jnp.broadcast_to(
        jnp.pad(counts.astype(F32), (0, 8 - slides), constant_values=1.0)[:, None], (8, 128)
    )

    line = Line()

    widths = (256, 256, 256, 128, 128)
    starts = [sum(widths[:q]) for q in range(len(widths))]
    generic = cell_bits != 3
    piece = min(shard, unit)
    keeps, steps, found, parts = {}, {}, {}, {}

    def make(*chunks, given=None):
        outs = predict(
            blocks_order,
            source,
            unit,
            piece,
            given,
            line(logits),
            starts[chunks[0]],
            tuple(widths[q] for q in chunks),
        )
        line.mark(outs[0])
        if given is not None:
            keeps[chunks[0] - 1], *outs = outs
        for n, q in enumerate(chunks):
            keeps[q] = outs[2 * n]
            found[q] = swap(outs[2 * n + 1], "cell", 0)

    def step(q):
        at = steps.get(q, 0)
        steps[q] = at + 1
        came = line(found[q])
        if at < cell_bits - 1:
            keeps[q], out = add_split(keeps[q], came)
            line.mark(out)
            found[q] = swap(out, "cell", at + 1)
        else:
            keeps[q] = stats(
                keeps[q], came, spatial, mask8, onehot, starts[q] // widths[q], widths[q]
            )
            line.mark(keeps[q][0])

    def own_exps():
        parts["m"] = exp_split(line(logits), False)
        line.mark(parts["m"][0])

    def other_exps():
        parts["p"] = exp_split(line(other_logits), False)
        line.mark(parts["p"][0])

    def masses():
        mass = mass_rows(line(sums), parts["m"])
        mass = jnp.concatenate([mass, jnp.broadcast_to(losses[0, 1], (8, 128))], axis=1)
        line.mark(mass)
        parts["mass"] = Total(line, mass, "spot", range(spots_n.bit_length() - 1))

    out, *first = predict(
        blocks_order, source, unit, piece, None, logits, 0, widths[:1], send_only=True
    )
    line.mark(out)
    found[0] = swap(out, "cell", 0)
    make(1, given=first)
    own_exps()
    if generic:
        make(2), make(3, 4), other_exps()
        for _ in range(cell_bits):
            for q in range(len(widths)):
                step(q)
    else:
        step(0), make(2), step(0), step(1), make(3, 4), step(0), step(2), step(1)
        other_exps(), step(2), step(3), step(1), step(4), step(3), step(2), step(4)
        step(3), step(4)
    number = len(widths)
    sums = jnp.concatenate([keeps[q][3] for q in range(number)], axis=1)
    mparts, pparts = parts["m"], parts["p"]
    preds = [keeps[q][0] for q in range(number)]
    spot_stats = [keeps[q][1] for q in range(number)]
    gene_stats = sum(keeps[q][2] for q in range(number))
    spot_stats = Total(line, jnp.concatenate(spot_stats, axis=1), "cell", range(cell_bits))
    gene_stats = Total(line, gene_stats, "spot", range(spots_n.bit_length() - 1))
    for _ in range(2):
        gene_stats.next(), spot_stats.next()
    gene_stats, spot_stats = gene_stats.end(), spot_stats.end()

    heights = (shard // 4,) * 4
    *grads, inner, losses = gradient(
        preds, sums, spatial, mask8, onehot, counts8, gene_stats, spot_stats, heights, slides, spots_total
    )

    blocks = spots_n // 2
    far_w = jnp.arange(blocks, dtype=jnp.int32)[:, None] << 1
    wanted = ((mine ^ far_w) * per_block + jnp.arange(per_block, dtype=jnp.int32)[None, :]) ^ me
    wanted = wanted.reshape(-1)
    place = reverse(wanted, cell_bits)
    low_bits = cell_bits - block_bits - 1
    short = ((place >> (low_bits + 1)) << low_bits) | (place & ((1 << low_bits) - 1))
    ids = jnp.concatenate([place, short]).astype(jnp.int32)
    core_bit = ((me >> block_bits) ^ mine) & 1

    line.mark(grads[0])
    number = len(heights)
    nears, fars, gots, acrosses, pairs, arrived = {}, {}, {}, {}, {}, {}

    def widen(q, bits):
        for bit in bits:
            if q in gots:
                nears[q] = glue(nears[q], line(gots[q]))
                line.mark(nears[q])
            else:
                nears[q] = line(nears[q])
            gots[q] = swap(nears[q], "cell", bit)

    def share(q):
        fars[q] = line(gots[q])
        size = heights[q] << low_bits
        out = pick(1 - core_bit.reshape(1), 1 << (block_bits - 1), size, nears[q], fars[q])
        line.mark(out)
        acrosses[q] = swap(out, "spot", 0)

    def multiply(q):
        outs = expr_part(
            ids, nears[q], fars[q], line(acrosses[q]), mparts, pparts, heights[q], blocks, wanted.size
        )
        outs = list(outs)
        line.mark(outs[0])
        bit = spots_n.bit_length() - 2
        while len(outs) > 2:
            half = len(outs) // 2
            came = swap(jnp.concatenate(outs[half:], axis=1), "spot", bit)
            came = jnp.split(came, half, axis=1)
            outs = [a + b for a, b in zip(outs[:half], came)]
            bit -= 1
        arrived[q] = swap(outs[1], "spot", bit)
        pairs[q] = (outs[0], arrived[q])

    nears.update(enumerate(grads))
    def first(q):
        widen(q, [cell_bits - 1])

    def second(q):
        widen(q, range(cell_bits - 2, 0, -1))

    def third(q):
        widen(q, [0])

    def pull():
        joint = parts["mass"].end()[:1]
        mass, parts["spots"] = joint[:, :rows] / spots_total, joint[0, rows]
        density_part = -jnp.sum(jnp.log(cells_total * mass)) / cells_total
        parts["dens"] = jnp.broadcast_to(-1.0 / (cells_total * spots_total * mass), (8, rows))
        added = inner + pull_cols(line(parts["dens"]), sums, mparts)
        added = jnp.concatenate(
            [added, jnp.broadcast_to(density_part - losses[0, 0], (8, 128))], axis=1
        )
        line.mark(added)
        parts["tail"] = Total(line, added, "cell", range(cell_bits - 1, -1, -1))

    def logits_of(chunks, ends, part, offset):
        grads_of = [v for q in chunks for v in (nears[q], fars[q])]
        size = [heights[q] for q in chunks]
        out = logit_part(
            order, ends, line(source), mparts, part, grads_of, size, offset, cells, unit, scale
        )
        line.mark(out)
        return out

    first(0), masses(), second(0), parts["mass"].next(), first(1), second(1), third(0), first(2)
    pull(), third(1), second(2), first(3), share(0), multiply(0), third(2), second(3)
    share(1), multiply(1), third(3), parts["tail"].next()
    line.also(arrived[0])
    share(2), multiply(2), parts["tail"].next()
    line.also(arrived[1])
    share(3)
    tail = parts["tail"].end()
    multiply(3)
    loss = tail[0, cols] - parts["spots"]
    pairs = [pairs[q] for q in range(number)]
    ends = parts["dens"], sums, tail[:, :cols]
    logit_grad = logits_of(range(number), ends, None, None)
    expr_grad = join(pairs, heights, per_block, scale)
    return (loss, logit_grad, expr_grad)


def solution(mesh):
    placed = (P("cell", "spot"), P("cell", None), P("cell", "spot"), P(), P("spot"), P())
    return jax.shard_map(
        on_device,
        mesh=mesh,
        in_specs=placed,
        out_specs=(P(), P("cell", "spot"), P("cell", "spot")),
        check_vma=False,
    )
```

```python
import functools

import jax
import jax.numpy as jnp
from jax import lax
from jax.experimental import pallas as pl
from jax.experimental.pallas import tpu as pltpu
from jax.sharding import PartitionSpec as P

eps = 1e-06
F32 = jnp.float32
BF16 = jnp.bfloat16
MIB = 1024 * 1024


def shape_of(*dims, dtype=F32):
    return jax.ShapeDtypeStruct(dims, dtype)


def hbm(*dims):
    return pltpu.HBM(dims[:-1], dims[-1])


def after(value, *others):
    return lax.optimization_barrier((value, *others))[0]


def params(mib):
    return pltpu.CompilerParams(vmem_limit_bytes=mib * MIB)


def split(v):
    high = v.astype(BF16)
    return high, (v - high.astype(F32)).astype(BF16)


def dot(a, b, ca, cb, precision=None):
    return lax.dot_general(
        a, b, (((ca,), (cb,)), ((), ())), precision=precision, preferred_element_type=F32
    )


def dot3(ah, al, bh, bl, ca, cb):
    return dot(ah, bh, ca, cb) + dot(al, bh, ca, cb) + dot(ah, bl, ca, cb)


def exact(a, b, ca, cb):
    return dot(a, b, ca, cb, lax.Precision.HIGHEST)


def cost(flops, nbytes):
    return pl.CostEstimate(flops=0, bytes_accessed=0, transcendentals=0)


def simple(body, outs, *args, prefetch=None):
    def spec(v):
        return pl.BlockSpec(v.shape, lambda i, *_: (0,) * len(v.shape))

    number = 0 if prefetch is None else 1
    return pl.pallas_call(
        body,
        grid_spec=pltpu.PrefetchScalarGridSpec(
            num_scalar_prefetch=number,
            grid=(1,),
            in_specs=[spec(a) for a in args],
            out_specs=[spec(o) for o in outs],
        ),
        out_shape=list(outs),
        compiler_params=params(32),
        cost_estimate=cost(0, 0),
    )(*([] if prefetch is None else [prefetch]), *args)


def add_body(a, b, out):
    out[...] = a[...] + b[...]


def add(a, b):
    return simple(add_body, [shape_of(*a.shape)], a, b)[0]


def add_split_body(kept, came, low, high):
    if len(kept.shape) == 3:
        low[...], high[...] = kept[0] + came[0], kept[1] + came[1]
    else:
        half = kept.shape[1] // 2
        low[...] = kept[:, :half] + came[:, :half]
        high[...] = kept[:, half:] + came[:, half:]


def add_split(kept, came):
    rows, cols = kept.shape[-2:]
    out = shape_of(rows, cols if kept.ndim == 3 else cols // 2)
    return simple(add_split_body, [out, out], kept, came)


def glue_body(*refs):
    *sources, out = refs
    at = 0
    for source in sources:
        out[at : at + source.shape[0], :] = source[...]
        at += source.shape[0]


def glue(*parts):
    return simple(glue_body, [shape_of(sum(p.shape[0] for p in parts), parts[0].shape[1])], *parts)[0]


def pick_body(outer, size, which, *refs):
    *sources, out = refs
    at = 0
    for source in sources:
        for n in range(outer):
            start = pl.multiple_of((2 * n + which[0]) * size, 8)
            out[at : at + size, :] = source[pl.ds(start, size), :]
            at += size


def pick(which, outer, size, *sources):
    out = shape_of(outer * size * len(sources), sources[0].shape[1])
    body = functools.partial(pick_body, outer, size)
    return simple(body, [out], *sources, prefetch=which)[0]


def exp_body(with_sums, logits, high, low, *sums):
    vals = jnp.exp(logits[...])
    high[...], low[...] = split(vals)
    if with_sums:

        @pl.when(pl.program_id(0) == 0)
        def _():
            sums[0][...] = jnp.zeros_like(sums[0])

        sums[0][...] += jnp.sum(vals.reshape(-1, 8, vals.shape[1]), axis=0)


def exp_split(logits, with_sums):
    rows, cols = logits.shape
    step = 1024
    tile = pl.BlockSpec((step, cols), lambda i: (i, 0))
    outs, shapes = [tile, tile], [hbm(rows, cols, BF16)] * 2
    if with_sums:
        outs += [pl.BlockSpec((8, cols), lambda i: (0, 0))]
        shapes += [shape_of(8, cols)]
    return pl.pallas_call(
        functools.partial(exp_body, with_sums),
        grid=(rows // step,),
        in_specs=[tile],
        out_specs=outs,
        out_shape=shapes,
        compiler_params=params(56),
        cost_estimate=cost(rows * cols * 10, rows * cols * 8),
    )(logits)


def mass_body(sums, mh, ml, out):
    inv = 1.0 / jnp.sum(sums[...], axis=0, keepdims=True)
    ih, il = split(jnp.broadcast_to(inv, (8, inv.shape[1])))
    out[...] = dot3(ih, il, mh[...], ml[...], 1, 1)


def mass_rows(sums, mparts):
    rows, cols = mparts[0].shape
    step = 1024
    tile = pl.BlockSpec((step, cols), lambda i: (i, 0))
    return pl.pallas_call(
        mass_body,
        grid=(rows // step,),
        in_specs=[pl.BlockSpec((8, cols), lambda i: (0, 0)), tile, tile],
        out_specs=pl.BlockSpec((8, step), lambda i: (0, i)),
        out_shape=shape_of(8, rows),
        compiler_params=params(56),
        cost_estimate=cost(rows * cols * 48, rows * cols * 4),
    )(sums, *mparts)


def below(total, shard, count):
    if total.shape[1] < shard:
        total = jnp.concatenate([total, jnp.zeros((1, shard - total.shape[1]), F32)], axis=1)
    lines = [total[:, at : at + shard] for at in range(0, total.shape[1], shard)]
    rows = jnp.concatenate(lines + [jnp.zeros((8 - len(lines), shard), F32)], axis=0)
    return jnp.concatenate([rows] * count, axis=1)


def predict_body(shard, given, widths, send_only, order, *refs):
    refs = list(refs)
    if given:
        gh, gl, gtotal = refs[:3]
        refs = refs[3:]
    if widths:
        logits, refs = refs[0], refs[1:]
    near = None if send_only else refs.pop(0)
    far = refs.pop(0) if widths else None
    if widths:
        total, refs = refs[-1], refs[:-1]
        th, tl, refs = refs[-2], refs[-1], refs[:-2]

        @pl.when(pl.program_id(0) == 0)
        def _():
            vals = jnp.exp(logits[...])
            total[...] = jnp.broadcast_to(jnp.sum(vals, axis=0, keepdims=True), total.shape)
            th[...], tl[...] = split(jnp.transpose(vals))

    count = (far if near is None else near).shape[1] // shard
    outs = iter(refs)
    if not send_only:
        near = split(near[...])
    if widths:
        far = split(far[...])
    if given:
        out, width = next(outs), gh.shape[0]
        out[:width] = dot3(gh[...], gl[...], *near, 1, 0)
        out[width:] = below(gtotal[:1], shard, count)
    if widths:
        kept = None if send_only else dot3(th[...], tl[...], *near, 1, 0)
        sent = dot3(th[...], tl[...], *far, 1, 0)
        at = 0
        for width in widths:
            rows = below(total[:1, at : at + width], shard, count)
            for vals in (kept, sent):
                if vals is not None:
                    out = next(outs)
                    out[:width] = vals[at : at + width]
                    out[width:] = rows
            at += width


def predict(order, expression, unit, shard, given, logits, start, widths, send_only=False):
    rows, genes = expression.shape
    count = genes // 2 // unit
    args, ins = [], []
    outs, shapes, scratch = [], [], []

    def add_out(width):
        outs.append(pl.BlockSpec((width + 8, unit), lambda i, order: (0, i)))
        shapes.append(shape_of(width + 8, genes // 2))

    if given is not None:
        width = given[0].shape[0]
        args += given
        ins += [pl.BlockSpec((width, rows), lambda i, order: (0, 0))] * 2
        ins += [pl.BlockSpec((8, width), lambda i, order: (0, 0))]
        add_out(width)
    wide = sum(widths)
    if widths:
        args.append(logits)
        ins.append(pl.BlockSpec((rows, wide), lambda i, order: (0, start // wide)))
        for width in widths:
            for _ in range(1 if send_only else 2):
                add_out(width)
    if not send_only:
        args.append(expression)
        ins.append(pl.BlockSpec((rows, unit), lambda i, order: (0, order[i])))
    if widths:
        args.append(expression)
        ins.append(pl.BlockSpec((rows, unit), lambda i, order: (0, order[count + i])))
        if send_only:
            outs += [pl.BlockSpec((wide, rows), lambda i, order: (0, 0))] * 2
            outs += [pl.BlockSpec((8, wide), lambda i, order: (0, 0))]
            shapes += [hbm(wide, rows, BF16)] * 2 + [shape_of(8, wide)]
        else:
            scratch = [pltpu.VMEM((wide, rows), BF16)] * 2 + [pltpu.VMEM((8, wide), F32)]
    return pl.pallas_call(
        functools.partial(predict_body, shard, given is not None, widths, send_only),
        grid_spec=pltpu.PrefetchScalarGridSpec(
            num_scalar_prefetch=1, grid=(count,), in_specs=ins, out_specs=outs, scratch_shapes=scratch
        ),
        out_shape=shapes,
        compiler_params=params(60),
        cost_estimate=cost(0, 0),
    )(order, *args)


def stats_body(width, kept, came, spatial, mask, onehot, pred, spots, genes, totals):
    vals = kept[...] + came[...]
    lines = max(1, width // vals.shape[1])
    total = jnp.concatenate([vals[width + n : width + n + 1] for n in range(lines)], axis=1)
    total = total[:, :width]
    totals[...] = jnp.concatenate([total, jnp.zeros((7, width), F32)], axis=0)
    vals = jnp.transpose(vals[:width]) / total
    pred[...] = vals
    spat = spatial[...]
    seen = dot(mask[...].astype(BF16), onehot[...].astype(BF16), 0, 0)
    terms = (vals * spat, vals * vals, spat * spat)
    rows = [jnp.sum(seen * t, axis=0, keepdims=True) for t in terms]
    spots[...] = jnp.concatenate(rows + [jnp.zeros((5, rows[0].shape[1]), F32)], axis=0)
    genes[...] = jnp.concatenate([exact(onehot[...], t, 1, 1) for t in terms], axis=0)


def stats(kept, came, spatial, mask, onehot, column, width):
    shard = kept.shape[1]
    strip = pl.BlockSpec((8, width), lambda i: (0, column))
    once = pl.BlockSpec((8, width), lambda i: (0, 0))
    given = pl.BlockSpec(kept.shape, lambda i: (0, 0))
    return pl.pallas_call(
        functools.partial(stats_body, width),
        grid=(1,),
        in_specs=[
            given,
            given,
            pl.BlockSpec((shard, width), lambda i: (0, column)),
            pl.BlockSpec((8, shard), lambda i: (0, 0)),
            strip,
        ],
        out_specs=[
            pl.BlockSpec((shard, width), lambda i: (0, 0)),
            once,
            pl.BlockSpec((24, shard), lambda i: (0, 0)),
            once,
        ],
        out_shape=[shape_of(shard, width), shape_of(8, width), shape_of(24, shard), shape_of(8, width)],
        compiler_params=params(32),
        cost_estimate=cost(0, 0),
    )(kept, came, spatial, mask, onehot)


def grad_body(slides, spots_total, parts, *refs):
    preds = refs[:parts]
    sums, spatial, mask, onehot, counts, gene_sums, spot_sums = refs[parts : parts + 7]
    outs = refs[parts + 7 : -2]
    inner, losses = refs[-2:]
    size = mask.shape[1]
    dot_g, pp_g, gg_g = (gene_sums[8 * i : 8 * i + 8, :] for i in range(3))
    norm_p, norm_s = jnp.sqrt(pp_g + eps), jnp.sqrt(gg_g + eps)
    weights = mask[...] / counts[...][:, :1]
    gene_part = jnp.sum(weights * (dot_g / (norm_p * norm_s))) / slides
    gene_weight = -weights / slides
    coef_s = gene_weight / (norm_p * norm_s)
    coef_p = gene_weight * dot_g / (norm_p * norm_p * norm_p * norm_s)
    a, b, c = (spot_sums[i : i + 1, :] for i in range(3))
    near_p, near_s = jnp.sqrt(b + eps), jnp.sqrt(c + eps)
    spot_part = jnp.sum(a / (near_p * near_s)) / spots_total
    edge_s = (-1.0 / spots_total) / (near_p * near_s)
    edge_p = (-1.0 / spots_total) * a / (near_p * near_p * near_p * near_s)
    total = jnp.sum(sums[...], axis=0, keepdims=True)
    hot = onehot[...]
    seen = dot(mask[...].astype(BF16), hot.astype(BF16), 0, 0)
    pred = jnp.concatenate([r[...] for r in preds], axis=1)
    grad = spatial[...] * (exact(coef_s, hot, 0, 0) + seen * edge_s) - pred * (
        exact(coef_p, hot, 0, 0) + seen * edge_p
    )
    row = jnp.sum(pred * grad, axis=0, keepdims=True)
    inner[...] = jnp.broadcast_to(row, inner.shape)
    grad = grad / total
    start = 0
    for out in outs:
        out[...] = grad[start : start + out.shape[0]]
        start += out.shape[0]
    lane = lax.broadcasted_iota(jnp.int32, losses.shape, 1)
    losses[...] = jnp.where(lane == 0, gene_part, jnp.where(lane == 1, spot_part, 0.0))


def gradient(preds, sums, spatial, mask, onehot, counts, gene_sums, spot_sums, heights, slides, spots_total):
    shard, cols = spatial.shape
    args = (*preds, sums, spatial, mask, onehot, counts, gene_sums, spot_sums)
    outs = [shape_of(h, cols) for h in heights] + [shape_of(8, cols), shape_of(8, 128)]
    return pl.pallas_call(
        functools.partial(grad_body, float(slides), float(spots_total), len(preds)),
        grid=(1,),
        in_specs=[pl.BlockSpec(a.shape, lambda i: (0, 0)) for a in args],
        out_specs=[pl.BlockSpec(o.shape, lambda i: (0, 0)) for o in outs],
        out_shape=outs,
        compiler_params=params(40),
        cost_estimate=cost(shard * cols * 60, shard * cols * 12),
    )(*args)


def pull_body(dens, sums, mh, ml, out):
    dh, dl = split(jnp.broadcast_to(dens[...][:1], dens.shape))

    @pl.when(pl.program_id(0) == 0)
    def _():
        out[...] = jnp.zeros_like(out)

    out[...] += dot3(dh, dl, mh[...], ml[...], 1, 0) / jnp.sum(sums[...], axis=0, keepdims=True)


def pull_cols(dens, sums, mparts):
    rows, cols = mparts[0].shape
    step = 1024
    tile = pl.BlockSpec((step, cols), lambda i: (i, 0))
    strip = pl.BlockSpec((8, cols), lambda i: (0, 0))
    return pl.pallas_call(
        pull_body,
        grid=(rows // step,),
        in_specs=[pl.BlockSpec((8, step), lambda i: (0, i)), strip, tile, tile],
        out_specs=strip,
        out_shape=shape_of(8, cols),
        compiler_params=params(56),
        cost_estimate=cost(rows * cols * 48, rows * cols * 4),
    )(dens, sums, *mparts)


def expr_body(number, height, half, ids, near, far, across, mh, ml, ph, pls, *refs):
    outs, (oh, ol, ch, cl) = refs[:-4], refs[-4:]

    @pl.when(pl.program_id(0) == 0)
    def _():
        for n in range(number):
            at = ids[n]
            inside = pl.ds(pl.multiple_of((at % half) * height, 16), height)
            own = jnp.where(at < half, near[inside, :], far[inside, :])
            other = across[pl.ds(pl.multiple_of(ids[number + n] * height, 16), height), :]
            put = slice(n * height, (n + 1) * height)
            oh[put, :], ol[put, :] = split(own)
            ch[put, :], cl[put, :] = split(other)

    vals = dot3(mh[...], ml[...], oh[...], ol[...], 1, 1) + dot3(
        ph[...], pls[...], ch[...], cl[...], 1, 1
    )
    width = vals.shape[1] // len(outs)
    for n, out in enumerate(outs):
        out[...] = vals[:, n * width : (n + 1) * width]


def expr_part(ids, near, far, across, mparts, pparts, height, blocks, number):
    rows, cols = mparts[0].shape
    step = 512
    half = near.shape[0] // height
    tile = pl.BlockSpec((step, cols), lambda i, ids: (i, 0))
    width = number * height // blocks
    return pl.pallas_call(
        functools.partial(expr_body, number, height, half),
        grid_spec=pltpu.PrefetchScalarGridSpec(
            num_scalar_prefetch=1,
            grid=(rows // step,),
            in_specs=[pl.BlockSpec(a.shape, lambda i, ids: (0, 0)) for a in (near, far, across)]
            + [tile] * 4,
            out_specs=[pl.BlockSpec((step, width), lambda i, ids: (i, 0))] * blocks,
            scratch_shapes=[pltpu.VMEM((number * height, cols), BF16)] * 4,
        ),
        out_shape=[shape_of(rows, width)] * blocks,
        compiler_params=params(48),
        cost_estimate=cost(12 * rows * cols * number * height, rows * cols * 8),
    )(ids, near, far, across, *mparts, *pparts)


def logit_body(pieces, heights, unit, offset, scale, final, added, order, *refs):
    if final:
        dens, sums, inner, *refs = refs
    source, mh, ml, *refs = refs
    if added:
        part, *refs = refs
    grads, (out, dh, dl) = refs[:-3], refs[-3:]
    high = sum(heights)

    @pl.when(pl.program_id(0) == 0)
    def _():
        for p in range(pieces):
            base = order[p] * high
            at = 0
            for q, height in enumerate(heights):
                grad = grads[2 * q + (p >= pieces // 2)]
                inside = p % (pieces // 2)
                rows = pl.ds(pl.multiple_of(base + at, 16), height)
                dh[rows, :], dl[rows, :] = split(grad[inside * height : (inside + 1) * height, :])
                at += height

    if offset is None:
        vals = source[...]
    else:
        vals = jnp.concatenate(
            [source[:, p * unit + offset : p * unit + offset + high] for p in range(pieces)], axis=1
        )
    vals = dot3(*split(vals), dh[...], dl[...], 1, 0)
    if added:
        vals = vals + part[...]
    if final:
        inv = 1.0 / jnp.sum(sums[...], axis=0, keepdims=True)
        column = jnp.transpose(dens[...])[:, :1]
        vals = vals + (column - inner[...][:1]) * inv
        vals = (mh[...].astype(F32) + ml[...].astype(F32)) * vals * scale
    out[...] = vals


def logit_part(order, ends, expression, mparts, part, grads, heights, offset, pieces, unit, scale):
    rows, cols = mparts[0].shape
    genes = expression.shape[1]
    step = 256
    strip = pl.BlockSpec((8, cols), lambda i, order: (0, 0))
    tile = pl.BlockSpec((step, cols), lambda i, order: (i, 0))
    added, final = part is not None, ends is not None
    ins = [pl.BlockSpec((step, genes), lambda i, order: (i, 0)), tile, tile]
    args = [expression, *mparts]
    if final:
        ins = [pl.BlockSpec((8, step), lambda i, order: (0, i)), strip, strip] + ins
        args = [*ends, *args]
    if added:
        ins.append(tile)
        args.append(part)
    for g in grads:
        ins.append(pl.BlockSpec(g.shape, lambda i, order: (0, 0), pipeline_mode=pl.Buffered(1)))
    return pl.pallas_call(
        functools.partial(logit_body, pieces, heights, unit, offset, scale, final, added),
        grid_spec=pltpu.PrefetchScalarGridSpec(
            num_scalar_prefetch=1,
            grid=(rows // step,),
            in_specs=ins,
            out_specs=tile,
            scratch_shapes=[pltpu.VMEM((pieces * sum(heights), cols), BF16)] * 2,
        ),
        out_shape=shape_of(rows, cols),
        compiler_params=params(56),
        cost_estimate=cost(0, 0),
    )(order, *args, *grads)


def join_body(shards, heights, scale, *refs):
    out = refs[-1]
    shard = sum(heights)
    at = 0
    for q, height in enumerate(heights):
        vals = (refs[2 * q][...] + refs[2 * q + 1][...]) * scale
        for b in range(shards):
            out[:, b * shard + at : b * shard + at + height] = vals[:, b * height : (b + 1) * height]
        at += height


def join(pairs, heights, shards, scale):
    flat = [v for pair in pairs for v in pair]
    rows = flat[0].shape[0]
    step = 1024
    genes = shards * sum(heights)
    return pl.pallas_call(
        functools.partial(join_body, shards, heights, scale),
        grid=(rows // step,),
        in_specs=[pl.BlockSpec((step, v.shape[1]), lambda i: (i, 0)) for v in flat],
        out_specs=pl.BlockSpec((step, genes), lambda i: (i, 0)),
        out_shape=shape_of(rows, genes),
        compiler_params=params(32),
        cost_estimate=cost(rows * genes * 2, rows * genes * 12),
    )(*flat)


class Line:
    def __init__(self):
        self.held = []

    def __call__(self, value):
        return after(value, *self.held) if self.held else value

    def mark(self, value):
        self.held = [value]

    def also(self, value):
        self.held = self.held + [value]


class Total:
    def __init__(self, line, value, axis, bits):
        self.line, self.value, self.axis, self.bits = line, value, axis, list(bits)
        self.come = swap(value, axis, self.bits.pop(0))

    def next(self):
        self.value = add(self.value, self.line(self.come))
        self.line.mark(self.value)
        self.come = swap(self.value, self.axis, self.bits.pop(0)) if self.bits else None

    def end(self):
        while self.come is not None:
            self.next()
        return self.value


def swap(v, axis, bit):
    size = lax.axis_size(axis)
    return lax.ppermute(v, axis, [(i, i ^ (1 << bit)) for i in range(size)])


def add_all(v, axis):
    for bit in range(lax.axis_size(axis).bit_length() - 1):
        v = add(v, swap(v, axis, bit))
    return v


def reverse(value, bits):
    return sum(((value >> b) & 1) << (bits - 1 - b) for b in range(bits))


def on_device(logits, expression, spatial, masks, slide_ids, counts):
    cells, spots_n = lax.axis_size("cell"), lax.axis_size("spot")
    me, mine = lax.axis_index("cell"), lax.axis_index("spot")
    rows, cols = logits.shape
    shard = spatial.shape[0]
    slides, genes = masks.shape
    cells_total, spots_total = rows * cells, cols * spots_n
    cell_bits = cells.bit_length() - 1
    per_block = cells // spots_n
    block_bits = per_block.bit_length() - 1
    scale = float(cells_total * spots_total)

    other_logits = swap(logits, "spot", 0)
    order = me ^ reverse(jnp.arange(cells, dtype=jnp.int32), cell_bits)
    unit = 256
    source, blocks_order = expression, order
    if shard != unit:
        source = source.reshape(rows, cells, shard)[:, order].reshape(rows, genes)
        blocks_order = jnp.arange(genes // unit, dtype=jnp.int32)
        order = jnp.arange(cells, dtype=jnp.int32)

    mask8 = jnp.pad(masks.astype(F32), ((0, 8 - slides), (0, 0)))
    mask8 = lax.dynamic_slice_in_dim(mask8, me * shard, shard, 1)
    onehot = (slide_ids[None, :] == jnp.arange(8, dtype=jnp.int32)[:, None]).astype(F32)
    counts8 = jnp.broadcast_to(
        jnp.pad(counts.astype(F32), (0, 8 - slides), constant_values=1.0)[:, None], (8, 128)
    )

    line = Line()

    widths = (256, 256, 256, 128, 128)
    starts = [sum(widths[:q]) for q in range(len(widths))]
    generic = cell_bits != 3
    piece = min(shard, unit)
    keeps, steps, found, parts = {}, {}, {}, {}

    def make(*chunks, given=None):
        outs = predict(
            blocks_order,
            source,
            unit,
            piece,
            given,
            line(logits),
            starts[chunks[0]],
            tuple(widths[q] for q in chunks),
        )
        line.mark(outs[0])
        if given is not None:
            keeps[chunks[0] - 1], *outs = outs
        for n, q in enumerate(chunks):
            keeps[q] = outs[2 * n]
            found[q] = swap(outs[2 * n + 1], "cell", 0)

    def step(q):
        at = steps.get(q, 0)
        steps[q] = at + 1
        came = line(found[q])
        if at < cell_bits - 1:
            keeps[q], out = add_split(keeps[q], came)
            line.mark(out)
            found[q] = swap(out, "cell", at + 1)
        else:
            keeps[q] = stats(
                keeps[q], came, spatial, mask8, onehot, starts[q] // widths[q], widths[q]
            )
            line.mark(keeps[q][0])

    def own_exps():
        parts["m"] = exp_split(line(logits), False)
        line.mark(parts["m"][0])

    def other_exps():
        parts["p"] = exp_split(line(other_logits), False)
        line.mark(parts["p"][0])

    def masses():
        mass = mass_rows(line(sums), parts["m"])
        mass = jnp.concatenate([mass, jnp.broadcast_to(losses[0, 1], (8, 128))], axis=1)
        line.mark(mass)
        parts["mass"] = Total(line, mass, "spot", range(spots_n.bit_length() - 1))

    out, *first = predict(
        blocks_order, source, unit, piece, None, logits, 0, widths[:1], send_only=True
    )
    line.mark(out)
    found[0] = swap(out, "cell", 0)
    make(1, given=first)
    own_exps()
    if generic:
        make(2), make(3, 4), other_exps()
        for _ in range(cell_bits):
            for q in range(len(widths)):
                step(q)
    else:
        step(0), make(2), step(0), step(1), make(3, 4), step(0), step(2), step(1)
        other_exps(), step(2), step(3), step(1), step(4), step(3), step(2), step(4)
        step(3), step(4)
    number = len(widths)
    sums = jnp.concatenate([keeps[q][3] for q in range(number)], axis=1)
    mparts, pparts = parts["m"], parts["p"]
    preds = [keeps[q][0] for q in range(number)]
    spot_stats = [keeps[q][1] for q in range(number)]
    gene_stats = sum(keeps[q][2] for q in range(number))
    spot_stats = Total(line, jnp.concatenate(spot_stats, axis=1), "cell", range(cell_bits))
    gene_stats = Total(line, gene_stats, "spot", range(spots_n.bit_length() - 1))
    for _ in range(2):
        gene_stats.next(), spot_stats.next()
    gene_stats, spot_stats = gene_stats.end(), spot_stats.end()

    heights = (shard // 4,) * 4
    *grads, inner, losses = gradient(
        preds, sums, spatial, mask8, onehot, counts8, gene_stats, spot_stats, heights, slides, spots_total
    )

    blocks = spots_n // 2
    far_w = jnp.arange(blocks, dtype=jnp.int32)[:, None] << 1
    wanted = ((mine ^ far_w) * per_block + jnp.arange(per_block, dtype=jnp.int32)[None, :]) ^ me
    wanted = wanted.reshape(-1)
    place = reverse(wanted, cell_bits)
    low_bits = cell_bits - block_bits - 1
    short = ((place >> (low_bits + 1)) << low_bits) | (place & ((1 << low_bits) - 1))
    ids = jnp.concatenate([place, short]).astype(jnp.int32)
    core_bit = ((me >> block_bits) ^ mine) & 1

    line.mark(grads[0])
    number = len(heights)
    nears, fars, gots, acrosses, pairs, arrived = {}, {}, {}, {}, {}, {}

    def widen(q, bits):
        for bit in bits:
            if q in gots:
                nears[q] = glue(nears[q], line(gots[q]))
                line.mark(nears[q])
            else:
                nears[q] = line(nears[q])
            gots[q] = swap(nears[q], "cell", bit)

    def share(q):
        fars[q] = line(gots[q])
        size = heights[q] << low_bits
        out = pick(1 - core_bit.reshape(1), 1 << (block_bits - 1), size, nears[q], fars[q])
        line.mark(out)
        acrosses[q] = swap(out, "spot", 0)

    def multiply(q):
        outs = expr_part(
            ids, nears[q], fars[q], line(acrosses[q]), mparts, pparts, heights[q], blocks, wanted.size
        )
        outs = list(outs)
        line.mark(outs[0])
        bit = spots_n.bit_length() - 2
        while len(outs) > 2:
            half = len(outs) // 2
            came = swap(jnp.concatenate(outs[half:], axis=1), "spot", bit)
            came = jnp.split(came, half, axis=1)
            outs = [a + b for a, b in zip(outs[:half], came)]
            bit -= 1
        arrived[q] = swap(outs[1], "spot", bit)
        pairs[q] = (outs[0], arrived[q])

    nears.update(enumerate(grads))
    def first(q):
        widen(q, [cell_bits - 1])

    def second(q):
        widen(q, range(cell_bits - 2, 0, -1))

    def third(q):
        widen(q, [0])

    def pull():
        joint = parts["mass"].end()[:1]
        mass, parts["spots"] = joint[:, :rows] / spots_total, joint[0, rows]
        density_part = -jnp.sum(jnp.log(cells_total * mass)) / cells_total
        parts["dens"] = jnp.broadcast_to(-1.0 / (cells_total * spots_total * mass), (8, rows))
        added = inner + pull_cols(line(parts["dens"]), sums, mparts)
        added = jnp.concatenate(
            [added, jnp.broadcast_to(density_part - losses[0, 0], (8, 128))], axis=1
        )
        line.mark(added)
        parts["tail"] = Total(line, added, "cell", range(cell_bits - 1, -1, -1))

    def logits_of(chunks, ends, part, offset):
        grads_of = [v for q in chunks for v in (nears[q], fars[q])]
        size = [heights[q] for q in chunks]
        out = logit_part(
            order, ends, line(source), mparts, part, grads_of, size, offset, cells, unit, scale
        )
        line.mark(out)
        return out

    first(0), masses(), second(0), parts["mass"].next(), first(1), second(1), third(0), first(2)
    pull(), third(1), second(2), first(3), share(0), multiply(0), third(2), second(3)
    share(1), multiply(1), third(3), parts["tail"].next()
    line.also(arrived[0])
    share(2), multiply(2), parts["tail"].next()
    line.also(arrived[1])
    share(3)
    tail = parts["tail"].end()
    multiply(3)
    loss = tail[0, cols] - parts["spots"]
    pairs = [pairs[q] for q in range(number)]
    ends = parts["dens"], sums, tail[:, :cols]
    logit_grad = logits_of(range(number), ends, None, None)
    expr_grad = join(pairs, heights, per_block, scale)
    return (loss, logit_grad, expr_grad)


def solution(mesh):
    placed = (P("cell", "spot"), P("cell", None), P("cell", "spot"), P(), P("spot"), P())
    return jax.shard_map(
        on_device,
        mesh=mesh,
        in_specs=placed,
        out_specs=(P(), P("cell", "spot"), P("cell", "spot")),
        check_vma=False,
    )
```

```python
import functools

import jax
import jax.numpy as jnp
from jax import lax
from jax.experimental import pallas as pl
from jax.experimental.pallas import tpu as pltpu
from jax.sharding import PartitionSpec as P

eps = 1e-06
F32 = jnp.float32
BF16 = jnp.bfloat16
MIB = 1024 * 1024


def shape_of(*dims, dtype=F32):
    return jax.ShapeDtypeStruct(dims, dtype)


def hbm(*dims):
    return pltpu.HBM(dims[:-1], dims[-1])


def after(value, *others):
    return lax.optimization_barrier((value, *others))[0]


def params(mib):
    return pltpu.CompilerParams(vmem_limit_bytes=mib * MIB)


def split(v):
    high = v.astype(BF16)
    return high, (v - high.astype(F32)).astype(BF16)


def dot(a, b, ca, cb, precision=None):
    return lax.dot_general(
        a, b, (((ca,), (cb,)), ((), ())), precision=precision, preferred_element_type=F32
    )


def dot3(ah, al, bh, bl, ca, cb):
    return dot(ah, bh, ca, cb) + dot(al, bh, ca, cb) + dot(ah, bl, ca, cb)


def exact(a, b, ca, cb):
    return dot(a, b, ca, cb, lax.Precision.HIGHEST)


def cost(flops, nbytes):
    return pl.CostEstimate(flops=0, bytes_accessed=0, transcendentals=0)


def simple(body, outs, *args, prefetch=None):
    def spec(v):
        return pl.BlockSpec(v.shape, lambda i, *_: (0,) * len(v.shape))

    number = 0 if prefetch is None else 1
    return pl.pallas_call(
        body,
        grid_spec=pltpu.PrefetchScalarGridSpec(
            num_scalar_prefetch=number,
            grid=(1,),
            in_specs=[spec(a) for a in args],
            out_specs=[spec(o) for o in outs],
        ),
        out_shape=list(outs),
        compiler_params=params(32),
        cost_estimate=cost(0, 0),
    )(*([] if prefetch is None else [prefetch]), *args)


def add_body(a, b, out):
    out[...] = a[...] + b[...]


def add(a, b):
    return simple(add_body, [shape_of(*a.shape)], a, b)[0]


def add_split_body(kept, came, low, high):
    if len(kept.shape) == 3:
        low[...], high[...] = kept[0] + came[0], kept[1] + came[1]
    else:
        half = kept.shape[1] // 2
        low[...] = kept[:, :half] + came[:, :half]
        high[...] = kept[:, half:] + came[:, half:]


def add_split(kept, came):
    rows, cols = kept.shape[-2:]
    out = shape_of(rows, cols if kept.ndim == 3 else cols // 2)
    return simple(add_split_body, [out, out], kept, came)


def glue_body(*refs):
    *sources, out = refs
    at = 0
    for source in sources:
        out[at : at + source.shape[0], :] = source[...]
        at += source.shape[0]


def glue(*parts):
    return simple(glue_body, [shape_of(sum(p.shape[0] for p in parts), parts[0].shape[1])], *parts)[0]


def pick_body(outer, size, which, *refs):
    *sources, out = refs
    at = 0
    for source in sources:
        for n in range(outer):
            start = pl.multiple_of((2 * n + which[0]) * size, 8)
            out[at : at + size, :] = source[pl.ds(start, size), :]
            at += size


def pick(which, outer, size, *sources):
    out = shape_of(outer * size * len(sources), sources[0].shape[1])
    body = functools.partial(pick_body, outer, size)
    return simple(body, [out], *sources, prefetch=which)[0]


def exp_body(with_sums, logits, high, low, *sums):
    vals = jnp.exp(logits[...])
    high[...], low[...] = split(vals)
    if with_sums:

        @pl.when(pl.program_id(0) == 0)
        def _():
            sums[0][...] = jnp.zeros_like(sums[0])

        sums[0][...] += jnp.sum(vals.reshape(-1, 8, vals.shape[1]), axis=0)


def exp_split(logits, with_sums):
    rows, cols = logits.shape
    step = 1024
    tile = pl.BlockSpec((step, cols), lambda i: (i, 0))
    outs, shapes = [tile, tile], [hbm(rows, cols, BF16)] * 2
    if with_sums:
        outs += [pl.BlockSpec((8, cols), lambda i: (0, 0))]
        shapes += [shape_of(8, cols)]
    return pl.pallas_call(
        functools.partial(exp_body, with_sums),
        grid=(rows // step,),
        in_specs=[tile],
        out_specs=outs,
        out_shape=shapes,
        compiler_params=params(56),
        cost_estimate=cost(rows * cols * 10, rows * cols * 8),
    )(logits)


def mass_body(sums, mh, ml, out):
    inv = 1.0 / jnp.sum(sums[...], axis=0, keepdims=True)
    ih, il = split(jnp.broadcast_to(inv, (8, inv.shape[1])))
    out[...] = dot3(ih, il, mh[...], ml[...], 1, 1)


def mass_rows(sums, mparts):
    rows, cols = mparts[0].shape
    step = 1024
    tile = pl.BlockSpec((step, cols), lambda i: (i, 0))
    return pl.pallas_call(
        mass_body,
        grid=(rows // step,),
        in_specs=[pl.BlockSpec((8, cols), lambda i: (0, 0)), tile, tile],
        out_specs=pl.BlockSpec((8, step), lambda i: (0, i)),
        out_shape=shape_of(8, rows),
        compiler_params=params(56),
        cost_estimate=cost(rows * cols * 48, rows * cols * 4),
    )(sums, *mparts)


def below(total, shard, count):
    if total.shape[1] < shard:
        total = jnp.concatenate([total, jnp.zeros((1, shard - total.shape[1]), F32)], axis=1)
    lines = [total[:, at : at + shard] for at in range(0, total.shape[1], shard)]
    rows = jnp.concatenate(lines + [jnp.zeros((8 - len(lines), shard), F32)], axis=0)
    return jnp.concatenate([rows] * count, axis=1)


def predict_body(shard, given, widths, send_only, order, *refs):
    refs = list(refs)
    if given:
        gh, gl, gtotal = refs[:3]
        refs = refs[3:]
    if widths:
        logits, refs = refs[0], refs[1:]
    near = None if send_only else refs.pop(0)
    far = refs.pop(0) if widths else None
    if widths:
        total, refs = refs[-1], refs[:-1]
        th, tl, refs = refs[-2], refs[-1], refs[:-2]

        @pl.when(pl.program_id(0) == 0)
        def _():
            vals = jnp.exp(logits[...])
            total[...] = jnp.broadcast_to(jnp.sum(vals, axis=0, keepdims=True), total.shape)
            th[...], tl[...] = split(jnp.transpose(vals))

    count = (far if near is None else near).shape[1] // shard
    outs = iter(refs)
    if not send_only:
        near = split(near[...])
    if widths:
        far = split(far[...])
    if given:
        out, width = next(outs), gh.shape[0]
        out[:width] = dot3(gh[...], gl[...], *near, 1, 0)
        out[width:] = below(gtotal[:1], shard, count)
    if widths:
        kept = None if send_only else dot3(th[...], tl[...], *near, 1, 0)
        sent = dot3(th[...], tl[...], *far, 1, 0)
        at = 0
        for width in widths:
            rows = below(total[:1, at : at + width], shard, count)
            for vals in (kept, sent):
                if vals is not None:
                    out = next(outs)
                    out[:width] = vals[at : at + width]
                    out[width:] = rows
            at += width


def predict(order, expression, unit, shard, given, logits, start, widths, send_only=False):
    rows, genes = expression.shape
    count = genes // 2 // unit
    args, ins = [], []
    outs, shapes, scratch = [], [], []

    def add_out(width):
        outs.append(pl.BlockSpec((width + 8, unit), lambda i, order: (0, i)))
        shapes.append(shape_of(width + 8, genes // 2))

    if given is not None:
        width = given[0].shape[0]
        args += given
        ins += [pl.BlockSpec((width, rows), lambda i, order: (0, 0))] * 2
        ins += [pl.BlockSpec((8, width), lambda i, order: (0, 0))]
        add_out(width)
    wide = sum(widths)
    if widths:
        args.append(logits)
        ins.append(pl.BlockSpec((rows, wide), lambda i, order: (0, start // wide)))
        for width in widths:
            for _ in range(1 if send_only else 2):
                add_out(width)
    if not send_only:
        args.append(expression)
        ins.append(pl.BlockSpec((rows, unit), lambda i, order: (0, order[i])))
    if widths:
        args.append(expression)
        ins.append(pl.BlockSpec((rows, unit), lambda i, order: (0, order[count + i])))
        if send_only:
            outs += [pl.BlockSpec((wide, rows), lambda i, order: (0, 0))] * 2
            outs += [pl.BlockSpec((8, wide), lambda i, order: (0, 0))]
            shapes += [hbm(wide, rows, BF16)] * 2 + [shape_of(8, wide)]
        else:
            scratch = [pltpu.VMEM((wide, rows), BF16)] * 2 + [pltpu.VMEM((8, wide), F32)]
    return pl.pallas_call(
        functools.partial(predict_body, shard, given is not None, widths, send_only),
        grid_spec=pltpu.PrefetchScalarGridSpec(
            num_scalar_prefetch=1, grid=(count,), in_specs=ins, out_specs=outs, scratch_shapes=scratch
        ),
        out_shape=shapes,
        compiler_params=params(60),
        cost_estimate=cost(0, 0),
    )(order, *args)


def stats_body(width, kept, came, spatial, mask, onehot, pred, spots, genes, totals):
    vals = kept[...] + came[...]
    lines = max(1, width // vals.shape[1])
    total = jnp.concatenate([vals[width + n : width + n + 1] for n in range(lines)], axis=1)
    total = total[:, :width]
    totals[...] = jnp.concatenate([total, jnp.zeros((7, width), F32)], axis=0)
    vals = jnp.transpose(vals[:width]) / total
    pred[...] = vals
    spat = spatial[...]
    seen = dot(mask[...].astype(BF16), onehot[...].astype(BF16), 0, 0)
    terms = (vals * spat, vals * vals, spat * spat)
    rows = [jnp.sum(seen * t, axis=0, keepdims=True) for t in terms]
    spots[...] = jnp.concatenate(rows + [jnp.zeros((5, rows[0].shape[1]), F32)], axis=0)
    genes[...] = jnp.concatenate([exact(onehot[...], t, 1, 1) for t in terms], axis=0)


def stats(kept, came, spatial, mask, onehot, column, width):
    shard = kept.shape[1]
    strip = pl.BlockSpec((8, width), lambda i: (0, column))
    once = pl.BlockSpec((8, width), lambda i: (0, 0))
    given = pl.BlockSpec(kept.shape, lambda i: (0, 0))
    return pl.pallas_call(
        functools.partial(stats_body, width),
        grid=(1,),
        in_specs=[
            given,
            given,
            pl.BlockSpec((shard, width), lambda i: (0, column)),
            pl.BlockSpec((8, shard), lambda i: (0, 0)),
            strip,
        ],
        out_specs=[
            pl.BlockSpec((shard, width), lambda i: (0, 0)),
            once,
            pl.BlockSpec((24, shard), lambda i: (0, 0)),
            once,
        ],
        out_shape=[shape_of(shard, width), shape_of(8, width), shape_of(24, shard), shape_of(8, width)],
        compiler_params=params(32),
        cost_estimate=cost(0, 0),
    )(kept, came, spatial, mask, onehot)


def grad_body(slides, spots_total, parts, *refs):
    preds = refs[:parts]
    sums, spatial, mask, onehot, counts, gene_sums, spot_sums = refs[parts : parts + 7]
    outs = refs[parts + 7 : -2]
    inner, losses = refs[-2:]
    size = mask.shape[1]
    dot_g, pp_g, gg_g = (gene_sums[8 * i : 8 * i + 8, :] for i in range(3))
    norm_p, norm_s = jnp.sqrt(pp_g + eps), jnp.sqrt(gg_g + eps)
    weights = mask[...] / counts[...][:, :1]
    gene_part = jnp.sum(weights * (dot_g / (norm_p * norm_s))) / slides
    gene_weight = -weights / slides
    coef_s = gene_weight / (norm_p * norm_s)
    coef_p = gene_weight * dot_g / (norm_p * norm_p * norm_p * norm_s)
    a, b, c = (spot_sums[i : i + 1, :] for i in range(3))
    near_p, near_s = jnp.sqrt(b + eps), jnp.sqrt(c + eps)
    spot_part = jnp.sum(a / (near_p * near_s)) / spots_total
    edge_s = (-1.0 / spots_total) / (near_p * near_s)
    edge_p = (-1.0 / spots_total) * a / (near_p * near_p * near_p * near_s)
    total = jnp.sum(sums[...], axis=0, keepdims=True)
    hot = onehot[...]
    seen = dot(mask[...].astype(BF16), hot.astype(BF16), 0, 0)
    pred = jnp.concatenate([r[...] for r in preds], axis=1)
    grad = spatial[...] * (exact(coef_s, hot, 0, 0) + seen * edge_s) - pred * (
        exact(coef_p, hot, 0, 0) + seen * edge_p
    )
    row = jnp.sum(pred * grad, axis=0, keepdims=True)
    inner[...] = jnp.broadcast_to(row, inner.shape)
    grad = grad / total
    start = 0
    for out in outs:
        out[...] = grad[start : start + out.shape[0]]
        start += out.shape[0]
    lane = lax.broadcasted_iota(jnp.int32, losses.shape, 1)
    losses[...] = jnp.where(lane == 0, gene_part, jnp.where(lane == 1, spot_part, 0.0))


def gradient(preds, sums, spatial, mask, onehot, counts, gene_sums, spot_sums, heights, slides, spots_total):
    shard, cols = spatial.shape
    args = (*preds, sums, spatial, mask, onehot, counts, gene_sums, spot_sums)
    outs = [shape_of(h, cols) for h in heights] + [shape_of(8, cols), shape_of(8, 128)]
    return pl.pallas_call(
        functools.partial(grad_body, float(slides), float(spots_total), len(preds)),
        grid=(1,),
        in_specs=[pl.BlockSpec(a.shape, lambda i: (0, 0)) for a in args],
        out_specs=[pl.BlockSpec(o.shape, lambda i: (0, 0)) for o in outs],
        out_shape=outs,
        compiler_params=params(40),
        cost_estimate=cost(shard * cols * 60, shard * cols * 12),
    )(*args)


def pull_body(dens, sums, mh, ml, out):
    dh, dl = split(jnp.broadcast_to(dens[...][:1], dens.shape))

    @pl.when(pl.program_id(0) == 0)
    def _():
        out[...] = jnp.zeros_like(out)

    out[...] += dot3(dh, dl, mh[...], ml[...], 1, 0) / jnp.sum(sums[...], axis=0, keepdims=True)


def pull_cols(dens, sums, mparts):
    rows, cols = mparts[0].shape
    step = 1024
    tile = pl.BlockSpec((step, cols), lambda i: (i, 0))
    strip = pl.BlockSpec((8, cols), lambda i: (0, 0))
    return pl.pallas_call(
        pull_body,
        grid=(rows // step,),
        in_specs=[pl.BlockSpec((8, step), lambda i: (0, i)), strip, tile, tile],
        out_specs=strip,
        out_shape=shape_of(8, cols),
        compiler_params=params(56),
        cost_estimate=cost(rows * cols * 48, rows * cols * 4),
    )(dens, sums, *mparts)


def expr_body(number, height, half, ids, near, far, across, mh, ml, ph, pls, *refs):
    outs, (oh, ol, ch, cl) = refs[:-4], refs[-4:]

    @pl.when(pl.program_id(0) == 0)
    def _():
        for n in range(number):
            at = ids[n]
            inside = pl.ds(pl.multiple_of((at % half) * height, 16), height)
            own = jnp.where(at < half, near[inside, :], far[inside, :])
            other = across[pl.ds(pl.multiple_of(ids[number + n] * height, 16), height), :]
            put = slice(n * height, (n + 1) * height)
            oh[put, :], ol[put, :] = split(own)
            ch[put, :], cl[put, :] = split(other)

    vals = dot3(mh[...], ml[...], oh[...], ol[...], 1, 1) + dot3(
        ph[...], pls[...], ch[...], cl[...], 1, 1
    )
    width = vals.shape[1] // len(outs)
    for n, out in enumerate(outs):
        out[...] = vals[:, n * width : (n + 1) * width]


def expr_part(ids, near, far, across, mparts, pparts, height, blocks, number):
    rows, cols = mparts[0].shape
    step = 512
    half = near.shape[0] // height
    tile = pl.BlockSpec((step, cols), lambda i, ids: (i, 0))
    width = number * height // blocks
    return pl.pallas_call(
        functools.partial(expr_body, number, height, half),
        grid_spec=pltpu.PrefetchScalarGridSpec(
            num_scalar_prefetch=1,
            grid=(rows // step,),
            in_specs=[pl.BlockSpec(a.shape, lambda i, ids: (0, 0)) for a in (near, far, across)]
            + [tile] * 4,
            out_specs=[pl.BlockSpec((step, width), lambda i, ids: (i, 0))] * blocks,
            scratch_shapes=[pltpu.VMEM((number * height, cols), BF16)] * 4,
        ),
        out_shape=[hbm(rows, width, F32)] * blocks,
        compiler_params=params(48),
        cost_estimate=cost(12 * rows * cols * number * height, rows * cols * 8),
    )(ids, near, far, across, *mparts, *pparts)


def logit_body(pieces, heights, unit, offset, scale, final, added, order, *refs):
    if final:
        dens, sums, inner, *refs = refs
    source, mh, ml, *refs = refs
    if added:
        part, *refs = refs
    grads, (out, dh, dl) = refs[:-3], refs[-3:]
    high = sum(heights)

    @pl.when(pl.program_id(0) == 0)
    def _():
        for p in range(pieces):
            base = order[p] * high
            at = 0
            for q, height in enumerate(heights):
                grad = grads[2 * q + (p >= pieces // 2)]
                inside = p % (pieces // 2)
                rows = pl.ds(pl.multiple_of(base + at, 16), height)
                dh[rows, :], dl[rows, :] = split(grad[inside * height : (inside + 1) * height, :])
                at += height

    if offset is None:
        vals = source[...]
    else:
        vals = jnp.concatenate(
            [source[:, p * unit + offset : p * unit + offset + high] for p in range(pieces)], axis=1
        )
    vals = dot3(*split(vals), dh[...], dl[...], 1, 0)
    if added:
        vals = vals + part[...]
    if final:
        inv = 1.0 / jnp.sum(sums[...], axis=0, keepdims=True)
        column = jnp.transpose(dens[...])[:, :1]
        vals = vals + (column - inner[...][:1]) * inv
        vals = (mh[...].astype(F32) + ml[...].astype(F32)) * vals * scale
    out[...] = vals


def logit_part(order, ends, expression, mparts, part, grads, heights, offset, pieces, unit, scale):
    rows, cols = mparts[0].shape
    genes = expression.shape[1]
    step = 256
    strip = pl.BlockSpec((8, cols), lambda i, order: (0, 0))
    tile = pl.BlockSpec((step, cols), lambda i, order: (i, 0))
    added, final = part is not None, ends is not None
    ins = [pl.BlockSpec((step, genes), lambda i, order: (i, 0)), tile, tile]
    args = [expression, *mparts]
    if final:
        ins = [pl.BlockSpec((8, step), lambda i, order: (0, i)), strip, strip] + ins
        args = [*ends, *args]
    if added:
        ins.append(tile)
        args.append(part)
    for g in grads:
        ins.append(pl.BlockSpec(g.shape, lambda i, order: (0, 0), pipeline_mode=pl.Buffered(1)))
    return pl.pallas_call(
        functools.partial(logit_body, pieces, heights, unit, offset, scale, final, added),
        grid_spec=pltpu.PrefetchScalarGridSpec(
            num_scalar_prefetch=1,
            grid=(rows // step,),
            in_specs=ins,
            out_specs=tile,
            scratch_shapes=[pltpu.VMEM((pieces * sum(heights), cols), BF16)] * 2,
        ),
        out_shape=shape_of(rows, cols),
        compiler_params=params(56),
        cost_estimate=cost(0, 0),
    )(order, *args, *grads)


def join_body(shards, heights, scale, *refs):
    out = refs[-1]
    shard = sum(heights)
    at = 0
    for q, height in enumerate(heights):
        vals = (refs[2 * q][...] + refs[2 * q + 1][...]) * scale
        for b in range(shards):
            out[:, b * shard + at : b * shard + at + height] = vals[:, b * height : (b + 1) * height]
        at += height


def join(pairs, heights, shards, scale):
    flat = [v for pair in pairs for v in pair]
    rows = flat[0].shape[0]
    step = 1024
    genes = shards * sum(heights)
    return pl.pallas_call(
        functools.partial(join_body, shards, heights, scale),
        grid=(rows // step,),
        in_specs=[pl.BlockSpec((step, v.shape[1]), lambda i: (i, 0)) for v in flat],
        out_specs=pl.BlockSpec((step, genes), lambda i: (i, 0)),
        out_shape=shape_of(rows, genes),
        compiler_params=params(32),
        cost_estimate=cost(rows * genes * 2, rows * genes * 12),
    )(*flat)


class Line:
    def __init__(self):
        self.held = []

    def __call__(self, value):
        return after(value, *self.held) if self.held else value

    def mark(self, value):
        self.held = [value]

    def also(self, value):
        self.held = self.held + [value]


class Total:
    def __init__(self, line, value, axis, bits):
        self.line, self.value, self.axis, self.bits = line, value, axis, list(bits)
        self.come = swap(value, axis, self.bits.pop(0))

    def next(self):
        self.value = add(self.value, self.line(self.come))
        self.line.mark(self.value)
        self.come = swap(self.value, self.axis, self.bits.pop(0)) if self.bits else None

    def end(self):
        while self.come is not None:
            self.next()
        return self.value


def swap(v, axis, bit):
    size = lax.axis_size(axis)
    return lax.ppermute(v, axis, [(i, i ^ (1 << bit)) for i in range(size)])


def add_all(v, axis):
    for bit in range(lax.axis_size(axis).bit_length() - 1):
        v = add(v, swap(v, axis, bit))
    return v


def reverse(value, bits):
    return sum(((value >> b) & 1) << (bits - 1 - b) for b in range(bits))


def on_device(logits, expression, spatial, masks, slide_ids, counts):
    cells, spots_n = lax.axis_size("cell"), lax.axis_size("spot")
    me, mine = lax.axis_index("cell"), lax.axis_index("spot")
    rows, cols = logits.shape
    shard = spatial.shape[0]
    slides, genes = masks.shape
    cells_total, spots_total = rows * cells, cols * spots_n
    cell_bits = cells.bit_length() - 1
    per_block = cells // spots_n
    block_bits = per_block.bit_length() - 1
    scale = float(cells_total * spots_total)

    other_logits = swap(logits, "spot", 0)
    order = me ^ reverse(jnp.arange(cells, dtype=jnp.int32), cell_bits)
    unit = 256
    source, blocks_order = expression, order
    if shard != unit:
        source = source.reshape(rows, cells, shard)[:, order].reshape(rows, genes)
        blocks_order = jnp.arange(genes // unit, dtype=jnp.int32)
        order = jnp.arange(cells, dtype=jnp.int32)

    mask8 = jnp.pad(masks.astype(F32), ((0, 8 - slides), (0, 0)))
    mask8 = lax.dynamic_slice_in_dim(mask8, me * shard, shard, 1)
    onehot = (slide_ids[None, :] == jnp.arange(8, dtype=jnp.int32)[:, None]).astype(F32)
    counts8 = jnp.broadcast_to(
        jnp.pad(counts.astype(F32), (0, 8 - slides), constant_values=1.0)[:, None], (8, 128)
    )

    line = Line()

    widths = (256, 256, 256, 128, 128)
    starts = [sum(widths[:q]) for q in range(len(widths))]
    generic = cell_bits != 3
    piece = min(shard, unit)
    keeps, steps, found, parts = {}, {}, {}, {}

    def make(*chunks, given=None):
        outs = predict(
            blocks_order,
            source,
            unit,
            piece,
            given,
            line(logits),
            starts[chunks[0]],
            tuple(widths[q] for q in chunks),
        )
        line.mark(outs[0])
        if given is not None:
            keeps[chunks[0] - 1], *outs = outs
        for n, q in enumerate(chunks):
            keeps[q] = outs[2 * n]
            found[q] = swap(outs[2 * n + 1], "cell", 0)

    def step(q):
        at = steps.get(q, 0)
        steps[q] = at + 1
        came = line(found[q])
        if at < cell_bits - 1:
            keeps[q], out = add_split(keeps[q], came)
            line.mark(out)
            found[q] = swap(out, "cell", at + 1)
        else:
            keeps[q] = stats(
                keeps[q], came, spatial, mask8, onehot, starts[q] // widths[q], widths[q]
            )
            line.mark(keeps[q][0])

    def own_exps():
        parts["m"] = exp_split(line(logits), False)
        line.mark(parts["m"][0])

    def other_exps():
        parts["p"] = exp_split(line(other_logits), False)
        line.mark(parts["p"][0])

    def masses():
        mass = mass_rows(line(sums), parts["m"])
        mass = jnp.concatenate([mass, jnp.broadcast_to(losses[0, 1], (8, 128))], axis=1)
        line.mark(mass)
        parts["mass"] = Total(line, mass, "spot", range(spots_n.bit_length() - 1))

    out, *first = predict(
        blocks_order, source, unit, piece, None, logits, 0, widths[:1], send_only=True
    )
    line.mark(out)
    found[0] = swap(out, "cell", 0)
    make(1, given=first)
    own_exps()
    if generic:
        make(2), make(3, 4), other_exps()
        for _ in range(cell_bits):
            for q in range(len(widths)):
                step(q)
    else:
        step(0), make(2), step(0), step(1), make(3, 4), step(0), step(2), step(1)
        other_exps(), step(2), step(3), step(1), step(4), step(3), step(2), step(4)
        step(3), step(4)
    number = len(widths)
    sums = jnp.concatenate([keeps[q][3] for q in range(number)], axis=1)
    mparts, pparts = parts["m"], parts["p"]
    preds = [keeps[q][0] for q in range(number)]
    spot_stats = [keeps[q][1] for q in range(number)]
    gene_stats = sum(keeps[q][2] for q in range(number))
    spot_stats = Total(line, jnp.concatenate(spot_stats, axis=1), "cell", range(cell_bits))
    gene_stats = Total(line, gene_stats, "spot", range(spots_n.bit_length() - 1))
    for _ in range(2):
        gene_stats.next(), spot_stats.next()
    gene_stats, spot_stats = gene_stats.end(), spot_stats.end()

    heights = (shard // 4,) * 4
    *grads, inner, losses = gradient(
        preds, sums, spatial, mask8, onehot, counts8, gene_stats, spot_stats, heights, slides, spots_total
    )

    blocks = spots_n // 2
    far_w = jnp.arange(blocks, dtype=jnp.int32)[:, None] << 1
    wanted = ((mine ^ far_w) * per_block + jnp.arange(per_block, dtype=jnp.int32)[None, :]) ^ me
    wanted = wanted.reshape(-1)
    place = reverse(wanted, cell_bits)
    low_bits = cell_bits - block_bits - 1
    short = ((place >> (low_bits + 1)) << low_bits) | (place & ((1 << low_bits) - 1))
    ids = jnp.concatenate([place, short]).astype(jnp.int32)
    core_bit = ((me >> block_bits) ^ mine) & 1

    line.mark(grads[0])
    number = len(heights)
    nears, fars, gots, acrosses, pairs, arrived = {}, {}, {}, {}, {}, {}

    def widen(q, bits):
        for bit in bits:
            if q in gots:
                nears[q] = glue(nears[q], line(gots[q]))
                line.mark(nears[q])
            else:
                nears[q] = line(nears[q])
            gots[q] = swap(nears[q], "cell", bit)

    def share(q):
        fars[q] = line(gots[q])
        size = heights[q] << low_bits
        out = pick(1 - core_bit.reshape(1), 1 << (block_bits - 1), size, nears[q], fars[q])
        line.mark(out)
        acrosses[q] = swap(out, "spot", 0)

    def multiply(q):
        outs = expr_part(
            ids, nears[q], fars[q], line(acrosses[q]), mparts, pparts, heights[q], blocks, wanted.size
        )
        outs = list(outs)
        line.mark(outs[0])
        bit = spots_n.bit_length() - 2
        while len(outs) > 2:
            half = len(outs) // 2
            came = swap(jnp.concatenate(outs[half:], axis=1), "spot", bit)
            came = jnp.split(came, half, axis=1)
            outs = [a + b for a, b in zip(outs[:half], came)]
            bit -= 1
        arrived[q] = swap(outs[1], "spot", bit)
        pairs[q] = (outs[0], arrived[q])

    nears.update(enumerate(grads))
    def first(q):
        widen(q, [cell_bits - 1])

    def second(q):
        widen(q, range(cell_bits - 2, 0, -1))

    def third(q):
        widen(q, [0])

    def pull():
        joint = parts["mass"].end()[:1]
        mass, parts["spots"] = joint[:, :rows] / spots_total, joint[0, rows]
        density_part = -jnp.sum(jnp.log(cells_total * mass)) / cells_total
        parts["dens"] = jnp.broadcast_to(-1.0 / (cells_total * spots_total * mass), (8, rows))
        added = inner + pull_cols(line(parts["dens"]), sums, mparts)
        added = jnp.concatenate(
            [added, jnp.broadcast_to(density_part - losses[0, 0], (8, 128))], axis=1
        )
        line.mark(added)
        parts["tail"] = Total(line, added, "cell", range(cell_bits - 1, -1, -1))

    def logits_of(chunks, ends, part, offset):
        grads_of = [v for q in chunks for v in (nears[q], fars[q])]
        size = [heights[q] for q in chunks]
        out = logit_part(
            order, ends, line(source), mparts, part, grads_of, size, offset, cells, unit, scale
        )
        line.mark(out)
        return out

    first(0), masses(), second(0), parts["mass"].next(), first(1), second(1), third(0), first(2)
    pull(), third(1), second(2), first(3), share(0), multiply(0), third(2), second(3)
    share(1), multiply(1), third(3), parts["tail"].next()
    line.also(arrived[0])
    share(2), multiply(2), parts["tail"].next()
    line.also(arrived[1])
    share(3)
    tail = parts["tail"].end()
    multiply(3)
    loss = tail[0, cols] - parts["spots"]
    pairs = [pairs[q] for q in range(number)]
    ends = parts["dens"], sums, tail[:, :cols]
    logit_grad = logits_of(range(number), ends, None, None)
    expr_grad = join(pairs, heights, per_block, scale)
    return (loss, logit_grad, expr_grad)


def solution(mesh):
    placed = (P("cell", "spot"), P("cell", None), P("cell", "spot"), P(), P("spot"), P())
    return jax.shard_map(
        on_device,
        mesh=mesh,
        in_specs=placed,
        out_specs=(P(), P("cell", "spot"), P("cell", "spot")),
        check_vma=False,
    )
```
